256 devices in a mesh: blk: 16 (over y_hi, x, core), dp: 16 (over z, y_lo).
Axes of the slice: x: 4, y: 4 (y_hi: 2, y_lo: 2; y = y_hi * 2 + y_lo), z: 8, core: 2. Of those that a mesh axis runs over, the one named last changes fastest.
Arguments:
- images: bfloat16 [65536, 1152], P(('blk', 'dp')), may hold values from -24 to 24
- texts: bfloat16 [65536, 1152], P(('blk', 'dp')), may hold values from -6 to 6
- head: bfloat16 [1152, 1152], replicated, may hold values from -0.1875 to 0.1875
- scale: float32 [1], replicated, may hold values from 4 to 12
- bias: float32 [1], replicated, may hold values from -3 to -1
Outputs:
- grad_image: float32 [65536, 1152], P(('blk', 'dp'))
- grad_text: float32 [65536, 1152], P(('blk', 'dp'))
- head_grad: float32 [1152, 1152], P('dp')
The draws below stay inside these ranges and needn't reach their ends.
All inputs are finite; a program needn't handle non-finite values.
Results may differ from the reference program's by a relative error of at most 0.012.
Values may be sent and summed in bfloat16 or wider, within the bound.
No kernel may reach another device: no remote copies, remote signals or barrier semaphores. Data moves between devices by JAX's collectives and lax.ppermute only.
A program may use at most 64 MiB of HBM per device.

```python
import jax
import jax.numpy as jnp
from jax import lax

D = 1152
E = 1152
TOK_DEV = 256
STEPS = 4
TOKENS = 65536
N_BLK = 16
N_DP = 16


def strengthened(drawn, key, source, target, shards_of, factor):
    def block_of(axis_at):
        return (jnp.arange(drawn.shape[axis_at]) // (drawn.shape[axis_at] // shards_of)).reshape((-1,) + (1,) * (drawn.ndim - 1 - axis_at))

    first = jax.random.permutation(key, shards_of)[block_of(target)]
    far = (block_of(target) + shards_of // 2) % shards_of
    return jnp.where((block_of(source) == first) | (block_of(source) == far), factor * drawn, drawn)


def steps_of(own_key, dims, shards, low, largest):
    factor_of, own = 1.0, jax.random.fold_in(own_key, 6)
    for position, shards_of in shards:
        heights = jnp.exp(jax.random.uniform(jax.random.fold_in(own, position), (shards_of,), jnp.float32, low / len(shards), largest / len(shards)))
        factor_of = factor_of * jnp.repeat(heights, dims[position] // shards_of).reshape([-1 if axis == position else 1 for axis in range(len(dims))])
    return factor_of


def normal_values(key, dims, width, limit, cuts=(), kind=jnp.bfloat16):
    result = width * jax.random.normal(key, dims, jnp.float32)
    if cuts:
        result = result * steps_of(key, dims, cuts, -0.22, 0.18)
    return jnp.clip(result, -limit, limit).astype(kind)


def bell_draw_with(stream_key, extent, spread, bound, split, heavy, kind=jnp.bfloat16):
    entries = spread * jax.random.normal(stream_key, extent, jnp.float32)
    if split:
        entries = entries * steps_of(stream_key, extent, split, -0.22, 0.18)
    return jnp.clip(strengthened(entries, jax.random.fold_in(stream_key, 3), *heavy), -bound, bound).astype(kind)


def setup_inputs(seed: int = 0) -> dict:
    key_of = jax.random.split(jax.random.key(seed), 6)
    return {
        "images": bell_draw_with(key_of[0], (TOKENS, D), 1.0, 24.0, ((0, 256),), (0, 1, 128, 5.5)),
        "texts": normal_values(key_of[1], (TOKENS, E), 1.0, 6.0, ((0, 256),)),
        "head": normal_values(key_of[2], (D, E), D ** -0.5, 0.1875),
        "scale": jnp.clip(jax.random.uniform(key_of[3], (1,), jnp.float32, 4.0, 12.0), 4.0, 12.0),
        "bias": jnp.clip(jax.random.uniform(key_of[4], (1,), jnp.float32, -3.0, -1.0), -3.0, -1.0),
    }


def reference(images, texts, head, scale, bias):
    scl = scale[0]
    bia = bias[0]
    proj = jnp.dot(images, head, preferred_element_type=jnp.float32)
    pnorm = jnp.sqrt(lax.optimization_barrier(jnp.sum(proj * proj, -1, keepdims=True)) + 1e-06)
    unit_img = proj / pnorm
    tfloat = texts.astype(jnp.float32)
    tnorm = jnp.sqrt(lax.optimization_barrier(jnp.sum(tfloat * tfloat, -1, keepdims=True)) + 1e-06)
    unit_txt = tfloat / tnorm
    img_b = unit_img.astype(jnp.bfloat16).astype(jnp.float32).reshape(N_BLK, N_DP, TOK_DEV, E)
    txt_b = unit_txt.astype(jnp.bfloat16).astype(jnp.float32).reshape(N_BLK, N_DP, TOK_DEV, E)
    eye = jnp.arange(TOK_DEV)[:, None] == jnp.arange(TOK_DEV)[None, :]
    dimg = jnp.zeros((N_BLK, N_DP, TOK_DEV, E), jnp.float32)
    dtxt = jnp.zeros((N_BLK, N_DP, TOK_DEV, E), jnp.float32)
    for step in range(STEPS + 1):
        moved = jnp.roll(txt_b, step, axis=0)
        logit = scl * jnp.einsum('bprk,bpqk->bprq', img_b, moved) + bia
        if step == 0:
            label = jnp.where(eye, 1.0, -1.0).astype(jnp.float32)
        else:
            label = -jnp.ones((TOK_DEV, TOK_DEV), jnp.float32)
        grad_b = (-label * jax.nn.sigmoid(-label * logit)).astype(jnp.bfloat16).astype(jnp.float32)
        dimg = dimg + scl * jnp.einsum('bprq,bpqk->bprk', grad_b, moved)
        part = scl * jnp.einsum('bprq,bprk->bpqk', grad_b, img_b)
        dtxt = dtxt + jnp.roll(part, -step, axis=0)
    dimg = dimg.reshape(TOKENS, E)
    dtxt = dtxt.reshape(TOKENS, E)
    grad_text = (dtxt - unit_txt * lax.optimization_barrier(jnp.sum(unit_txt * dtxt, -1, keepdims=True))) / tnorm
    dproj_b = ((dimg - unit_img * lax.optimization_barrier(jnp.sum(unit_img * dimg, -1, keepdims=True))) / pnorm).astype(jnp.bfloat16)
    grad_image = jnp.dot(dproj_b, head.T, preferred_element_type=jnp.float32)
    head_grad = jnp.dot(images.T, dproj_b, preferred_element_type=jnp.float32) / jnp.sqrt(jnp.float32(TOKENS))
    return (grad_image, grad_text, head_grad)
```

```python
import jax
import jax.numpy as jnp
from jax import lax
from jax.sharding import Mesh, PartitionSpec as P

AXES = ("yh", "x", "core", "z", "yl")
SIZES = (2, 4, 2, 8, 2)
BF = jnp.bfloat16
F32 = jnp.float32


def chip_pairs(steps):
    _, xs, cores, zs, yls = SIZES
    inner = zs * yls
    count = 16 * inner
    shift = steps * cores * inner
    return [(source, (source + shift) % count) for source in range(count)]


def core_pairs():
    inner = SIZES[3] * SIZES[4]
    return [(source, source ^ inner) for source in range(16 * inner)]


def moved(value, pairs):
    return lax.ppermute(value, AXES, pairs)


def mm(a, b, dims):
    return lax.dot_general(a, b, ((dims[:1], dims[1:]), ((), ())), preferred_element_type=F32)


def on_device(images, texts, head, scale, bias):
    scl = scale[0]
    bia = bias[0]
    core = lax.axis_index("core")
    first = core == 0
    ahead, back, swap = chip_pairs(1), chip_pairs(-1), core_pairs()

    tfloat = texts.astype(F32)
    tnorm = jnp.sqrt(jnp.sum(tfloat * tfloat, -1, keepdims=True) + 1e-06)
    unit_txt = tfloat / tnorm
    txt_b = unit_txt.astype(BF)
    t1 = moved(txt_b, ahead)
    proj = jnp.dot(images, head, preferred_element_type=F32)
    pnorm = jnp.sqrt(jnp.sum(proj * proj, -1, keepdims=True) + 1e-06)
    unit_img = proj / pnorm
    img_b = unit_img.astype(BF)
    i1 = moved(img_b, back)
    images2 = moved(images, swap)
    r1 = moved(jnp.where(first, txt_b, img_b), swap)

    def pair_grad(rows, cols):
        logit = scl * mm(rows, cols, (1, 1)) + bia
        return jax.nn.sigmoid(logit).astype(BF)

    def applied(rows, cols):
        return mm(pair_grad(rows, cols), cols, (1, 0))

    count = images.shape[0]
    eye = lax.broadcasted_iota(jnp.int32, (count, count), 0) == lax.broadcasted_iota(
        jnp.int32, (count, count), 1
    )
    logit = scl * mm(img_b, txt_b, (1, 1)) + bia
    g0 = jnp.where(eye, -jax.nn.sigmoid(-logit), jax.nn.sigmoid(logit)).astype(BF)
    dimg = mm(g0, txt_b, (1, 0))
    dtxt = mm(g0, img_b, (0, 0))

    a1 = applied(jnp.where(first, txt_b, img_b), r1)
    dimg = dimg + jnp.where(first, 0.0, a1)
    dtxt = dtxt + jnp.where(first, a1, 0.0)

    t2 = moved(t1, ahead)
    i2 = moved(i1, back)
    t1s = moved(t1, swap)
    i1s = moved(i1, swap)
    dimg = dimg + applied(img_b, t1) + applied(img_b, t1s)
    dtxt = dtxt + applied(txt_b, i1) + applied(txt_b, i1s)

    r3 = moved(jnp.where(first, i2, t2), swap)
    dimg = dimg + applied(img_b, t2)
    dtxt = dtxt + applied(txt_b, i2)
    a3 = applied(jnp.where(first, img_b, txt_b), r3)
    dimg = scl * (dimg + jnp.where(first, a3, 0.0))
    dtxt = scl * (dtxt + jnp.where(first, 0.0, a3))

    dproj_b = ((dimg - unit_img * jnp.sum(unit_img * dimg, -1, keepdims=True)) / pnorm).astype(BF)

    width = images.shape[1]
    half = width // 2
    low, high = dproj_b[:, :half], dproj_b[:, half:]
    mine = jnp.where(first, low, high)
    other = moved(jnp.where(first, high, low), swap)
    part = mm(
        jnp.concatenate([mine, other], 0), jnp.concatenate([images, images2], 0), (0, 0)
    ).astype(BF)
    chips = SIZES[0] * SIZES[1]
    piece = half // chips
    part = lax.all_to_all(part.reshape(chips, piece, width), ("yh", "x"), 0, 0)
    part = jnp.sum(part.astype(F32), 0).astype(BF)
    dps = SIZES[3] * SIZES[4]
    own = width // dps
    part = part.reshape(piece, dps, own).transpose(1, 0, 2)
    part = lax.all_to_all(part, ("z", "yl"), 0, 0)
    part = jnp.sum(part.astype(F32), 0).astype(BF)
    blks = chips * SIZES[2]
    whole = lax.all_to_all(jnp.broadcast_to(part[None], (blks, piece, own)), ("yh", "x", "core"), 0, 0)
    order = whole.reshape(chips, SIZES[2], piece, own).transpose(3, 1, 0, 2).reshape(own, width)
    total_pairs = count * 256
    head_grad = order.astype(F32) * (1.0 / jnp.sqrt(jnp.float32(total_pairs)))

    grad_image = mm(dproj_b, head, (1, 1))
    grad_text = (dtxt - unit_txt * jnp.sum(unit_txt * dtxt, -1, keepdims=True)) / tnorm
    return (grad_image, grad_text, head_grad)


def solution(mesh):
    fine = Mesh(mesh.devices.reshape(SIZES), AXES)
    rows = P(AXES, None)
    return jax.shard_map(
        on_device,
        mesh=fine,
        in_specs=(rows, rows, P(), P(), P()),
        out_specs=(rows, rows, P(("z", "yl"), None)),
        check_vma=False,
    )
```

```python
import functools

import jax
import jax.numpy as jnp
from jax import lax
from jax.experimental import pallas as pl
from jax.experimental.pallas import tpu as pltpu
from jax.sharding import Mesh, PartitionSpec as P

AXES = ("yh", "x", "core", "z", "yl")
SIZES = (2, 4, 2, 8, 2)
INNER = SIZES[3] * SIZES[4]
COUNT = 16 * INNER
CHIPS = SIZES[0] * SIZES[1]
BLKS = CHIPS * SIZES[2]
BF = jnp.bfloat16
F32 = jnp.float32


def chip_pairs(steps):
    shift = steps * SIZES[2] * INNER
    return [(source, (source + shift) % COUNT) for source in range(COUNT)]


def core_pairs(only=None):
    return [
        (source, source ^ INNER)
        for source in range(COUNT)
        if only is None or (source // INNER) % 2 == only
    ]


def moved(value, pairs):
    return lax.ppermute(value, AXES, pairs)


def mm(a, b, dims):
    return lax.dot_general(a, b, ((dims[:1], dims[1:]), ((), ())), preferred_element_type=F32)


def call(body, outs, *args, scalars=(), pairs=0.0):
    in_specs = [pl.BlockSpec(memory_space=pltpu.SMEM)] * len(scalars)
    in_specs += [pl.BlockSpec(memory_space=pltpu.VMEM)] * len(args)
    return pl.pallas_call(
        body,
        out_shape=[jax.ShapeDtypeStruct(shape, dtype) for shape, dtype in outs],
        in_specs=in_specs,
        out_specs=[pl.BlockSpec(memory_space=pltpu.VMEM)] * len(outs),
        cost_estimate=pl.CostEstimate(
            flops=int(pairs * 3.02e8),
            bytes_accessed=sum(int(a.size) * a.dtype.itemsize for a in args),
            transcendentals=0,
        ),
        compiler_params=pltpu.CompilerParams(vmem_limit_bytes=32 * 2**20),
    )(*scalars, *args)


def sigmoid(x):
    return 1.0 / (1.0 + jnp.exp(-x))


def applied(par, rows, cols):
    logit = par[0] * mm(rows, cols, (1, 1)) + par[1]
    return mm(sigmoid(logit).astype(BF), cols, (1, 0))


def text_unit(texts):
    tfloat = texts.astype(F32)
    tnorm = jnp.sqrt(jnp.sum(tfloat * tfloat, -1, keepdims=True) + 1e-06)
    return tfloat / tnorm, tnorm


def text_body(texts, out):
    out[...] = text_unit(texts[...])[0].astype(BF)


def image_body(core, images, head, txt_b, unit, norm, img_b, mixed):
    proj = jnp.dot(images[...], head[...], preferred_element_type=F32)
    pnorm = jnp.sqrt(jnp.sum(proj * proj, -1, keepdims=True) + 1e-06)
    value = proj / pnorm
    unit[...] = value
    norm[...] = pnorm
    low = value.astype(BF)
    img_b[...] = low

    @pl.when(core[0] == 0)
    def _():
        mixed[...] = txt_b[...]

    @pl.when(core[0] != 0)
    def _():
        mixed[...] = low


def home_body(par, core, img_b, txt_b, r1, dimg, dtxt):
    logit = par[0] * mm(img_b[...], txt_b[...], (1, 1)) + par[1]
    eye = lax.broadcasted_iota(jnp.int32, logit.shape, 0) == lax.broadcasted_iota(
        jnp.int32, logit.shape, 1
    )
    away = sigmoid(logit)
    grad = jnp.where(eye, -sigmoid(-logit), away).astype(BF)
    dimg[...] = mm(grad, txt_b[...], (1, 0))
    dtxt[...] = mm(grad, img_b[...], (0, 0))

    @pl.when(core[0] == 0)
    def _():
        dtxt[...] += applied(par, txt_b[...], r1[...])

    @pl.when(core[0] != 0)
    def _():
        dimg[...] += applied(par, img_b[...], r1[...])


def two_body(par, own, near, nears, old, new):
    new[...] = old[...] + applied(par, own[...], near[...]) + applied(par, own[...], nears[...])


def one_body(par, own, near, old, new):
    new[...] = old[...] + applied(par, own[...], near[...])


def image_end_body(par, core, img_b, r3, old, unit, norm, whole, keep, send, total):
    total[...] = old[...]

    @pl.when(core[0] == 0)
    def _():
        total[...] += applied(par, img_b[...], r3[...])

    dimg = par[0] * total[...]
    value = unit[...]
    dproj = ((dimg - value * jnp.sum(value * dimg, -1, keepdims=True)) / norm[...]).astype(BF)
    whole[...] = dproj
    half = dproj.shape[1] // 2

    @pl.when(core[0] == 0)
    def _():
        keep[...] = dproj[:, :half]
        send[...] = dproj[:, half:]

    @pl.when(core[0] != 0)
    def _():
        keep[...] = dproj[:, half:]
        send[...] = dproj[:, :half]


def head_body(keep, other, images, images2, out):
    total = mm(keep[...], images[...], (0, 0)) + mm(other[...], images2[...], (0, 0))
    out[...] = total.astype(BF).reshape(out.shape)


def text_end_body(par, core, txt_b, i2, r3, old, texts, out):
    out[...] = old[...] + applied(par, txt_b[...], i2[...])

    @pl.when(core[0] != 0)
    def _():
        out[...] += applied(par, txt_b[...], r3[...])

    dtxt = par[0] * out[...]
    value, tnorm = text_unit(texts[...])
    out[...] = (dtxt - value * jnp.sum(value * dtxt, -1, keepdims=True)) / tnorm


def grad_image_body(dproj, head, out):
    out[...] = mm(dproj[...], head[...], (1, 1))


def added(ref):
    total = ref[0].astype(F32)
    for k in range(1, ref.shape[0]):
        total = total + ref[k].astype(F32)
    return total


def split_body(parts, out):
    total = added(parts)
    own = out.shape[2]
    for k in range(out.shape[0]):
        out[k] = total[:, k * own : (k + 1) * own].astype(BF)


def spread_body(parts, out):
    total = added(parts).astype(BF)
    for k in range(out.shape[0]):
        out[k] = total


def join_body(factor, parts, out):
    cores = SIZES[2]
    pieces = [
        parts[chip * cores + core].astype(F32) for core in range(cores) for chip in range(CHIPS)
    ]
    out[...] = jnp.concatenate(pieces, 0).T * factor


def on_device(images, texts, head, scale, bias):
    par = jnp.concatenate([scale, bias])
    core = lax.axis_index("core").astype(jnp.int32).reshape(1)
    ahead, back, swap = chip_pairs(1), chip_pairs(-1), core_pairs()
    count, width = images.shape
    half = width // 2
    big = (count, width)

    (txt_b,) = call(text_body, [(big, BF)], texts, pairs=1)
    t1 = moved(txt_b, ahead)
    unit_img, pnorm, img_b, mixed = call(
        image_body,
        [(big, F32), ((count, 1), F32), (big, BF), (big, BF)],
        images, head, txt_b, scalars=(core,), pairs=4,
    )
    i1 = moved(img_b, back)
    images2 = moved(images, swap)
    r1 = moved(mixed, swap)
    dimg, dtxt = call(home_body, [(big, F32)] * 2, img_b, txt_b, r1, scalars=(par, core), pairs=3)

    t2 = moved(t1, ahead)
    i2 = moved(i1, back)
    t1s = moved(t1, swap)
    i1s = moved(i1, swap)
    (dimg,) = call(two_body, [(big, F32)], img_b, t1, t1s, dimg, scalars=(par,), pairs=2)
    (dtxt,) = call(two_body, [(big, F32)], txt_b, i1, i1s, dtxt, scalars=(par,), pairs=2)

    r3t = moved(t2, core_pairs(1))
    r3i = moved(i2, core_pairs(0))
    (dimg,) = call(one_body, [(big, F32)], img_b, t2, dimg, scalars=(par,), pairs=1)
    dproj, keep, send = call(
        image_end_body,
        [(big, BF), ((count, half), BF), ((count, half), BF), (big, F32)],
        img_b, r3t, dimg, unit_img, pnorm, scalars=(par, core), pairs=2,
    )[:3]
    other = moved(send, swap)
    piece = half // CHIPS
    (part,) = call(head_body, [((CHIPS, piece, width), BF)], keep, other, images, images2, pairs=2)
    part = lax.all_to_all(part, ("yh", "x"), 0, 0)
    own = width // INNER
    (grad_text,) = call(
        text_end_body, [(big, F32)], txt_b, i2, r3i, dtxt, texts, scalars=(par, core), pairs=3
    )
    (grad_image,) = call(grad_image_body, [(big, F32)], dproj, head, pairs=2)
    (part,) = call(split_body, [((INNER, piece, own), BF)], part)
    part = lax.all_to_all(part, ("z", "yl"), 0, 0)
    (part,) = call(spread_body, [((BLKS, piece, own), BF)], part)
    part = lax.all_to_all(part, ("yh", "x", "core"), 0, 0)
    factor = 1.0 / float(count * COUNT) ** 0.5
    (head_grad,) = call(functools.partial(join_body, factor), [((own, width), F32)], part)
    return (grad_image, grad_text, head_grad)


def solution(mesh):
    fine = Mesh(mesh.devices.reshape(SIZES), AXES)
    rows = P(AXES, None)
    return jax.shard_map(
        on_device,
        mesh=fine,
        in_specs=(rows, rows, P(), P(), P()),
        out_specs=(rows, rows, P(("z", "yl"), None)),
        check_vma=False,
    )
```

```python
import functools

import jax
import jax.numpy as jnp
import numpy as np
from jax import lax
from jax.experimental import pallas as pl
from jax.experimental.pallas import tpu as pltpu
from jax.sharding import Mesh, PartitionSpec as P

AXES = ("yh", "x", "core", "z", "yl")
SIZES = (2, 4, 2, 8, 2)
INNER = SIZES[3] * SIZES[4]
COUNT = 16 * INNER
CHIPS = SIZES[0] * SIZES[1]
BLKS = CHIPS * SIZES[2]
BF = jnp.bfloat16
F32 = jnp.float32


def chip_pairs(steps):
    shift = steps * SIZES[2] * INNER
    return [(source, (source + shift) % COUNT) for source in range(COUNT)]


def core_pairs(only=None):
    return [
        (source, source ^ INNER)
        for source in range(COUNT)
        if only is None or (source // INNER) % 2 == only
    ]


def moved(value, pairs):
    return lax.ppermute(value, AXES, pairs)


def mm(a, b, dims):
    return lax.dot_general(a, b, ((dims[:1], dims[1:]), ((), ())), preferred_element_type=F32)


def call(body, outs, *args, scalars=(), pairs=0.0, scratch=(), space=pltpu.VMEM):
    in_specs = [pl.BlockSpec(memory_space=pltpu.SMEM)] * len(scalars)
    in_specs += [pl.BlockSpec(memory_space=space)] * len(args)
    return pl.pallas_call(
        body,
        out_shape=[jax.ShapeDtypeStruct(shape, dtype) for shape, dtype in outs],
        in_specs=in_specs,
        out_specs=[pl.BlockSpec(memory_space=pltpu.VMEM)] * len(outs),
        scratch_shapes=list(scratch),
        cost_estimate=pl.CostEstimate(
            flops=int(pairs * 3.02e8),
            bytes_accessed=sum(int(a.size) * a.dtype.itemsize for a in args),
            transcendentals=0,
        ),
        compiler_params=pltpu.CompilerParams(vmem_limit_bytes=32 * 2**20),
    )(*scalars, *args)


def sigmoid(x):
    return 1.0 / (1.0 + jnp.exp(-x))


def applied(par, rows, cols):
    logit = par[0] * mm(rows, cols, (1, 1)) + par[1]
    return mm(sigmoid(logit).astype(BF), cols, (1, 0))


def text_unit(texts):
    tfloat = texts.astype(F32)
    tnorm = jnp.sqrt(jnp.sum(tfloat * tfloat, -1, keepdims=True) + 1e-06)
    inverse = 1.0 / tnorm
    return tfloat * inverse, inverse


CUTS = (0, 256, 512, 768, 1152)


def start_body(core, images, texts, head, txt_b, unit, norm, img_b, mixed, t_in, i_in, h_in, sems):
    copies = [
        pltpu.make_async_copy(texts, t_in, sems.at[0]),
        pltpu.make_async_copy(images, i_in, sems.at[1]),
    ]
    for k in range(len(CUTS) - 1):
        rows = pl.ds(CUTS[k], CUTS[k + 1] - CUTS[k])
        copies.append(pltpu.make_async_copy(head.at[rows], h_in.at[rows], sems.at[2 + k]))
    for copy in copies:
        copy.start()
    copies[0].wait()
    low_txt = text_unit(t_in[...])[0].astype(BF)
    txt_b[...] = low_txt
    copies[1].wait()
    proj = None
    for k in range(len(CUTS) - 1):
        copies[2 + k].wait()
        cut = slice(CUTS[k], CUTS[k + 1])
        term = jnp.dot(i_in[:, cut], h_in[cut, :], preferred_element_type=F32)
        proj = term if proj is None else proj + term
    pnorm = jnp.sqrt(jnp.sum(proj * proj, -1, keepdims=True) + 1e-06)
    inverse = 1.0 / pnorm
    value = proj * inverse
    unit[...] = value
    norm[...] = inverse
    low = value.astype(BF)
    img_b[...] = low

    @pl.when(core[0] == 0)
    def _():
        mixed[...] = low_txt

    @pl.when(core[0] != 0)
    def _():
        mixed[...] = low


def order_body(images, out):
    own = images.shape[1] // INNER
    for z in range(SIZES[3]):
        for yl in range(SIZES[4]):
            source, target = (z * SIZES[4] + yl) * own, (yl * SIZES[3] + z) * own
            out[:, target : target + own] = images[:, source : source + own]


def home_body(par, core, img_b, txt_b, r1, dimg, dtxt):
    logit = par[0] * mm(img_b[...], txt_b[...], (1, 1)) + par[1]
    eye = lax.broadcasted_iota(jnp.int32, logit.shape, 0) == lax.broadcasted_iota(
        jnp.int32, logit.shape, 1
    )
    away = sigmoid(logit)
    grad = jnp.where(eye, -sigmoid(-logit), away).astype(BF)
    dimg[...] = mm(grad, txt_b[...], (1, 0))
    dtxt[...] = mm(grad, img_b[...], (0, 0))

    @pl.when(core[0] == 0)
    def _():
        dtxt[...] += applied(par, txt_b[...], r1[...])

    @pl.when(core[0] != 0)
    def _():
        dimg[...] += applied(par, img_b[...], r1[...])


def near_body(par, img_b, txt_b, t1, t1s, i1, i1s, dimg, dtxt, dimg_out, dtxt_out):
    dimg_out[...] = dimg[...] + applied(par, img_b[...], t1[...]) + applied(par, img_b[...], t1s[...])
    dtxt_out[...] = dtxt[...] + applied(par, txt_b[...], i1[...]) + applied(par, txt_b[...], i1s[...])


def one_body(par, own, near, old, new):
    new[...] = old[...] + applied(par, own[...], near[...])


def image_end_body(par, core, img_b, r3, old, unit, norm, whole, keep, send, total):
    total[...] = old[...]

    @pl.when(core[0] == 0)
    def _():
        total[...] += applied(par, img_b[...], r3[...])

    dimg = par[0] * total[...]
    value = unit[...]
    dproj = ((dimg - value * jnp.sum(value * dimg, -1, keepdims=True)) * norm[...]).astype(BF)
    whole[...] = dproj
    half = dproj.shape[1] // 2

    @pl.when(core[0] == 0)
    def _():
        keep[...] = dproj[:, :half]
        send[...] = dproj[:, half:]

    @pl.when(core[0] != 0)
    def _():
        keep[...] = dproj[:, half:]
        send[...] = dproj[:, :half]


TURNS = (0, 1, 3, 2)


def turned(place, pieces, outs):
    for turn, out in zip(TURNS, outs):
        out[...] = pieces[lax.rem(place[0] + turn, 4)]


def head_body(core, place, keep, other, images, images2, *rest):
    outs, pieces = rest[:4], rest[4]
    total = mm(keep[...], images[...], (0, 0)) + mm(other[...], images2[...], (0, 0))
    rows, half = pieces.shape[1], total.shape[1] // 2

    @pl.when(core[0] == 0)
    def _():
        for k in range(4):
            pieces[k] = total[k * rows : (k + 1) * rows].astype(BF)

    @pl.when(core[0] != 0)
    def _():
        for k in range(4):
            up, left = 2 * (k // 2) * rows, (k % 2) * half
            first = total[up : up + rows, left : left + half]
            second = total[up + rows : up + 2 * rows, left : left + half]
            pieces[k] = jnp.concatenate([first, second], 1).astype(BF)

    turned(place, pieces, outs)


def quarter_body(core, place, a, b, c, d, *rest):
    outs, pieces = rest[:4], rest[4]
    total = a[...].astype(F32) + b[...].astype(F32) + c[...].astype(F32) + d[...].astype(F32)
    _, rows, half = pieces.shape

    def quadrant(down, right):
        return total[down * rows : (down + 1) * rows, right * half : (right + 1) * half].astype(BF)

    @pl.when(core[0] == 0)
    def _():
        for k in range(4):
            pieces[k] = quadrant(k // 2, k % 2)

    @pl.when(core[0] != 0)
    def _():
        for k in range(4):
            pieces[k] = quadrant(k % 2, k // 2)

    turned(place, pieces, outs)


def text_end_body(par, core, txt_b, i2, r3, old, texts, out):
    out[...] = old[...] + applied(par, txt_b[...], i2[...])

    @pl.when(core[0] != 0)
    def _():
        out[...] += applied(par, txt_b[...], r3[...])

    dtxt = par[0] * out[...]
    value, inverse = text_unit(texts[...])
    out[...] = (dtxt - value * jnp.sum(value * dtxt, -1, keepdims=True)) * inverse


def grad_image_body(dproj, head, out):
    out[...] = mm(dproj[...], head[...], (1, 1))


def split_body(a, b, c, d, out):
    total = a[...].astype(F32) + b[...].astype(F32) + c[...].astype(F32) + d[...].astype(F32)
    own = out.shape[2]
    for k in range(out.shape[0]):
        out[k] = total[:, k * own : (k + 1) * own].astype(BF)


def spread_body(parts, out):
    total = parts[0].astype(F32)
    for k in range(1, parts.shape[0]):
        total = total + parts[k].astype(F32)
    total = total.astype(BF)
    for k in range(out.shape[0]):
        out[k] = total


def join_body(factor, parts, out):
    yhs, xs, cores = SIZES[:3]
    order = [(yh * xs + x) * cores for x in range(xs) for yh in range(yhs)]
    order += [(yh * xs + x) * cores + 1 for yh in range(yhs) for x in range(xs)]
    out[...] = jnp.concatenate([parts[k].astype(F32) for k in order], 0).T * factor


def ring_pairs(turn, first):
    pairs = []
    for source in range(COUNT):
        yh, x, core, z, yl = np.unravel_index(source, SIZES)
        if core == first:
            x = (x + turn) % SIZES[1]
        else:
            y = (yh * SIZES[4] + yl + turn) % 4
            yh, yl = y // SIZES[4], y % SIZES[4]
        pairs.append((source, int(np.ravel_multi_index((yh, x, core, z, yl), SIZES))))
    return pairs


def on_device(images, texts, head, scale, bias):
    par = jnp.concatenate([scale, bias])
    core = lax.axis_index("core").astype(jnp.int32).reshape(1)
    across = lax.axis_index("x").astype(jnp.int32).reshape(1)
    along = lax.axis_index(("yh", "yl")).astype(jnp.int32).reshape(1)
    place_a = jnp.where(core == 0, across, along)
    place_b = jnp.where(core == 0, along, across)
    ahead, back, swap = chip_pairs(1), chip_pairs(-1), core_pairs()
    count, width = images.shape
    half = width // 2
    big = (count, width)
    tie = lax.optimization_barrier

    txt_b, unit_img, pnorm, img_b, mixed = call(
        start_body,
        [(big, BF), (big, F32), ((count, 1), F32), (big, BF), (big, BF)],
        images, texts, head, scalars=(core,), pairs=6, space=pltpu.HBM,
        scratch=[
            pltpu.VMEM(big, BF), pltpu.VMEM(big, BF), pltpu.VMEM(head.shape, BF),
            pltpu.SemaphoreType.DMA((1 + len(CUTS),)),
        ],
    )
    t1 = moved(txt_b, ahead)
    i1 = moved(img_b, back)
    r1 = moved(mixed, swap)
    dimg, dtxt = call(home_body, [(big, F32)] * 2, img_b, txt_b, r1, scalars=(par, core), pairs=6)
    (ordered,) = call(order_body, [(big, BF)], images, pairs=2)

    t2 = moved(t1, ahead)
    i2 = moved(i1, back)
    t1x, i1x, dimg, dtxt, ordered = tie((t1, i1, dimg, dtxt, ordered))
    t1s = moved(t1x, swap)
    i1s = moved(i1x, swap)
    ordered2 = moved(ordered, swap)
    dimg, dtxt = call(
        near_body, [(big, F32)] * 2, img_b, txt_b, t1x, t1s, i1x, i1s, dimg, dtxt,
        scalars=(par,), pairs=8,
    )
    t2, dimg, dtxt, ordered2 = tie((t2, dimg, dtxt, ordered2))

    r3t = moved(t2, core_pairs(1))
    (dimg,) = call(one_body, [(big, F32)], img_b, t2, dimg, scalars=(par,), pairs=3)
    dproj, keep, send = call(
        image_end_body,
        [(big, BF), ((count, half), BF), ((count, half), BF), (big, F32)],
        img_b, r3t, dimg, unit_img, pnorm, scalars=(par, core), pairs=6,
    )[:3]
    other = moved(send, swap)
    quarter = ((half // 4, width), BF)
    parts = call(
        head_body, [quarter] * 4, keep, other, ordered, ordered2, scalars=(core, place_a), pairs=3,
        scratch=[pltpu.VMEM((4, half // 4, width), BF)],
    )
    parts = list(parts[:1]) + [moved(p, ring_pairs(t, 0)) for p, t in zip(parts[1:], TURNS[1:])]
    (grad_image,) = call(grad_image_body, [(big, F32)], dproj, head, pairs=6)
    i2 = tie((i2, keep))[0]
    r3i = moved(i2, core_pairs(0))
    small = ((half // 8, half), BF)
    parts = call(
        quarter_body, [small] * 4, *parts, scalars=(core, place_b), pairs=1,
        scratch=[pltpu.VMEM((4, half // 8, half), BF)],
    )
    parts = list(parts[:1]) + [moved(p, ring_pairs(t, 1)) for p, t in zip(parts[1:], TURNS[1:])]
    (grad_text,) = call(
        text_end_body, [(big, F32)], txt_b, i2, r3i, dtxt, texts, scalars=(par, core), pairs=8
    )
    own = width // INNER
    (part,) = call(split_body, [((SIZES[3], half // 8, own), BF)], *parts)
    part = lax.all_to_all(part, "z", 0, 0)
    (part,) = call(spread_body, [((BLKS, half // 8, own), BF)], part)
    part = lax.all_to_all(part, ("yh", "x", "core"), 0, 0)
    factor = 1.0 / float(count * COUNT) ** 0.5
    (head_grad,) = call(functools.partial(join_body, factor), [((own, width), F32)], part)
    return (grad_image, grad_text, head_grad)


def solution(mesh):
    fine = Mesh(mesh.devices.reshape(SIZES), AXES)
    rows = P(AXES, None)
    return jax.shard_map(
        on_device,
        mesh=fine,
        in_specs=(rows, rows, P(), P(), P()),
        out_specs=(rows, rows, P(("z", "yl"), None)),
        check_vma=False,
    )
```

```python
import functools

import jax
import jax.numpy as jnp
import numpy as np
from jax import lax
from jax.experimental import pallas as pl
from jax.experimental.pallas import tpu as pltpu
from jax.sharding import Mesh, PartitionSpec as P

AXES = ("yh", "x", "core", "z", "yl")
SIZES = (2, 4, 2, 8, 2)
INNER = SIZES[3] * SIZES[4]
COUNT = 16 * INNER
CHIPS = SIZES[0] * SIZES[1]
BLKS = CHIPS * SIZES[2]
BF = jnp.bfloat16
F32 = jnp.float32


def chip_pairs(steps):
    shift = steps * SIZES[2] * INNER
    return [(source, (source + shift) % COUNT) for source in range(COUNT)]


def core_pairs(only=None):
    return [
        (source, source ^ INNER)
        for source in range(COUNT)
        if only is None or (source // INNER) % 2 == only
    ]


def moved(value, pairs):
    return lax.ppermute(value, AXES, pairs)


def mm(a, b, dims):
    return lax.dot_general(a, b, ((dims[:1], dims[1:]), ((), ())), preferred_element_type=F32)


def call(body, outs, *args, scalars=(), scratch=(), limit=8, space=pltpu.VMEM, small=0):
    in_specs = [pl.BlockSpec(memory_space=pltpu.SMEM)] * len(scalars)
    in_specs += [pl.BlockSpec(memory_space=space)] * len(args)
    shapes = [jax.ShapeDtypeStruct(shape, dtype) for shape, dtype in outs]
    if space is pltpu.HBM:
        args = [pltpu.with_memory_space_constraint(a, space) for a in args]
    return pl.pallas_call(
        body,
        out_shape=shapes,
        in_specs=in_specs,
        out_specs=[pl.BlockSpec(memory_space=pltpu.SMEM)] * small
        + [pl.BlockSpec(memory_space=pltpu.VMEM)] * (len(outs) - small),
        scratch_shapes=list(scratch),
        cost_estimate=pl.CostEstimate(
            flops=0,
            bytes_accessed=sum(int(np.prod(a.shape)) * a.dtype.itemsize for a in (*args, *shapes)),
            transcendentals=0,
        ),
        compiler_params=pltpu.CompilerParams(vmem_limit_bytes=limit * 2**20),
    )(*scalars, *args)


def sigmoid(x):
    return 1.0 / (1.0 + jnp.exp(-x))


def applied(par, rows, cols):
    logit = par[0] * mm(rows, cols, (1, 1)) + par[1]
    return mm(sigmoid(logit).astype(BF), cols, (1, 0))


def text_unit(texts):
    tfloat = texts.astype(F32)
    tnorm = jnp.sqrt(jnp.sum(tfloat * tfloat, -1, keepdims=True) + 1e-06)
    inverse = 1.0 / tnorm
    return tfloat * inverse, inverse


def halved(value, first, second):
    rows = value.shape[0] // 2
    first[...] = value[:rows]
    second[...] = value[rows:]


CUTS = (0, 256, 512, 768, 1152)


def start_body(
    here, scale, bias, images, texts, head, info, par,
    ta, tb, ia, ib, both, unit, norm, t_in, i_in, h_in, sems,
):
    copies = [
        pltpu.make_async_copy(texts, t_in, sems.at[0]),
        pltpu.make_async_copy(images, i_in, sems.at[1]),
    ]
    for k in range(len(CUTS) - 1):
        rows = pl.ds(CUTS[k], CUTS[k + 1] - CUTS[k])
        copies.append(pltpu.make_async_copy(head.at[rows], h_in.at[rows], sems.at[2 + k]))
    for copy in copies:
        copy.start()
    for k in range(here.shape[0]):
        info[k] = here[k]
    par[0] = scale[0]
    par[1] = bias[0]
    copies[0].wait()
    count = t_in.shape[0]
    low = text_unit(t_in[...])[0].astype(BF)
    halved(low, ta, tb)
    both[:count] = low
    copies[1].wait()
    both[2 * count :] = i_in[...]
    proj = None
    for k in range(len(CUTS) - 1):
        copies[2 + k].wait()
        cut = slice(CUTS[k], CUTS[k + 1])
        term = jnp.dot(i_in[:, cut], h_in[cut, :], preferred_element_type=F32)
        proj = term if proj is None else proj + term
    inverse = 1.0 / jnp.sqrt(jnp.sum(proj * proj, -1, keepdims=True) + 1e-06)
    value = proj * inverse
    unit[...] = value
    norm[...] = inverse
    low = value.astype(BF)
    halved(low, ia, ib)
    both[count : 2 * count] = low


def text_of(both):
    return both[: both.shape[0] // 3]


def image_of(both):
    count = both.shape[0] // 3
    return both[count : 2 * count]


def order_body(both, both_s, out, out2):
    own = both.shape[1] // INNER
    count = both.shape[0] // 3
    for z in range(SIZES[3]):
        for yl in range(SIZES[4]):
            source, target = (z * SIZES[4] + yl) * own, (yl * SIZES[3] + z) * own
            out[:, target : target + own] = both[2 * count :, source : source + own]
            out2[:, target : target + own] = both_s[2 * count :, source : source + own]


def home_body(par, both, dimg, dtxt):
    img_b, txt_b = image_of(both), text_of(both)
    logit = par[0] * mm(img_b, txt_b, (1, 1)) + par[1]
    eye = lax.broadcasted_iota(jnp.int32, logit.shape, 0) == lax.broadcasted_iota(
        jnp.int32, logit.shape, 1
    )
    grad = jnp.where(eye, -sigmoid(-logit), sigmoid(logit)).astype(BF)
    dimg[...] = mm(grad, txt_b, (1, 0))
    dtxt[...] = mm(grad, img_b, (0, 0))


def joined(first, second):
    return jnp.concatenate([first[...], second[...]], 0)


def near_body(par, core, t1a, t1b, i1a, i1b, both, both_s, dimg, dtxt, dimg_o, dtxt_o, dimg_s, dtxt_s):
    t1, i1 = joined(t1a, t1b), joined(i1a, i1b)
    dimg_o[...] = dimg[...] + applied(par, image_of(both), t1)
    dtxt_o[...] = dtxt[...] + applied(par, text_of(both), i1)
    dimg_s[...] = applied(par, image_of(both_s), t1)
    dtxt_s[...] = applied(par, text_of(both_s), i1)

    @pl.when(core[0] == 0)
    def _():
        dtxt_o[...] += applied(par, text_of(both), image_of(both_s))

    @pl.when(core[0] != 0)
    def _():
        dimg_o[...] += applied(par, image_of(both), text_of(both_s))


def give_body(giver, rows_of, par, core, first, second, both_s, old, out):
    @pl.when(core[0] == giver)
    def _():
        out[...] = (old[...] + applied(par, rows_of(both_s), joined(first, second))).astype(BF)

    @pl.when(core[0] != giver)
    def _():
        out[...] = old[...].astype(BF)


def far_body(rows_of, par, first, second, both, old, out):
    out[...] = old[...] + applied(par, rows_of(both), joined(first, second))


def image_end_body(par, core, old, given, unit, norm, whole, keep, send):
    dimg = par[0] * (old[...] + given[...].astype(F32))
    value = unit[...]
    dproj = ((dimg - value * jnp.sum(value * dimg, -1, keepdims=True)) * norm[...]).astype(BF)
    whole[...] = dproj
    half = dproj.shape[1] // 2

    @pl.when(core[0] == 0)
    def _():
        keep[...] = dproj[:, :half]
        send[...] = dproj[:, half:]

    @pl.when(core[0] != 0)
    def _():
        keep[...] = dproj[:, half:]
        send[...] = dproj[:, :half]


def text_end_body(par, old, given, texts, out):
    dtxt = par[0] * (old[...] + given[...].astype(F32))
    value, inverse = text_unit(texts[...])
    out[...] = (dtxt - value * jnp.sum(value * dtxt, -1, keepdims=True)) * inverse


TURNS = (0, 1, 3, 2)


def turned(place, pieces, outs):
    for turn, out in zip(TURNS, outs):
        out[...] = pieces[lax.rem(place + turn, 4)]


def head_body(core, keep, other, images, images2, *rest):
    outs, pieces = rest[:4], rest[4]
    total = mm(keep[...], images[...], (0, 0)) + mm(other[...], images2[...], (0, 0))
    rows, half = pieces.shape[1], total.shape[1] // 2

    @pl.when(core[0] == 0)
    def _():
        for k in range(4):
            pieces[k] = total[k * rows : (k + 1) * rows].astype(BF)

    @pl.when(core[0] != 0)
    def _():
        for k in range(4):
            up, left = 2 * (k // 2) * rows, (k % 2) * half
            first = total[up : up + rows, left : left + half]
            second = total[up + rows : up + 2 * rows, left : left + half]
            pieces[k] = jnp.concatenate([first, second], 1).astype(BF)

    turned(core[1], pieces, outs)


def quarter_body(core, a, b, c, d, *rest):
    outs, pieces = rest[:4], rest[4]
    total = a[...].astype(F32) + b[...].astype(F32) + c[...].astype(F32) + d[...].astype(F32)
    _, rows, half = pieces.shape

    def quadrant(down, right):
        return total[down * rows : (down + 1) * rows, right * half : (right + 1) * half].astype(BF)

    @pl.when(core[0] == 0)
    def _():
        for k in range(4):
            pieces[k] = quadrant(k // 2, k % 2)

    @pl.when(core[0] != 0)
    def _():
        for k in range(4):
            pieces[k] = quadrant(k % 2, k // 2)

    turned(core[2], pieces, outs)


def grad_image_body(dproj, head, out):
    out[...] = mm(dproj[...], head[...], (1, 1))


def split_body(a, b, c, d, out):
    total = a[...].astype(F32) + b[...].astype(F32) + c[...].astype(F32) + d[...].astype(F32)
    own = out.shape[2]
    for k in range(out.shape[0]):
        out[k] = total[:, k * own : (k + 1) * own].astype(BF)


def spread_body(parts, out):
    total = parts[0].astype(F32)
    for k in range(1, parts.shape[0]):
        total = total + parts[k].astype(F32)
    total = total.astype(BF)
    for k in range(out.shape[0]):
        out[k] = total


def join_body(factor, parts, out):
    yhs, xs, cores = SIZES[:3]
    order = [(yh * xs + x) * cores for x in range(xs) for yh in range(yhs)]
    order += [(yh * xs + x) * cores + 1 for yh in range(yhs) for x in range(xs)]
    out[...] = jnp.concatenate([parts[k].astype(F32) for k in order], 0).T * factor


def ring_pairs(turn, first):
    pairs = []
    for source in range(COUNT):
        yh, x, core, z, yl = np.unravel_index(source, SIZES)
        if core == first:
            x = (x + turn) % SIZES[1]
        else:
            y = (yh * SIZES[4] + yl + turn) % 4
            yh, yl = y // SIZES[4], y % SIZES[4]
        pairs.append((source, int(np.ravel_multi_index((yh, x, core, z, yl), SIZES))))
    return pairs


def on_device(images, texts, head, scale, bias):
    core = lax.axis_index("core")
    across, along = lax.axis_index("x"), lax.axis_index(("yh", "yl"))
    here = jnp.stack(
        [core, jnp.where(core == 0, across, along), jnp.where(core == 0, along, across)]
    ).astype(jnp.int32)
    ahead, back, swap = chip_pairs(1), chip_pairs(-1), core_pairs()
    count, width = images.shape
    half = width // 2
    big = (count, width)
    tie = lax.optimization_barrier

    part_of = ((count // 2, width), BF)
    info, par, ta, tb, ia, ib, both, unit_img, pnorm = call(
        start_body,
        [((3,), jnp.int32), ((2,), F32)] + [part_of] * 4 + [((3 * count, width), BF), (big, F32), ((count, 1), F32)],
        images, texts, head, scalars=(here, scale, bias), small=2, space=pltpu.HBM, limit=16,
        scratch=[
            pltpu.VMEM(big, BF), pltpu.VMEM(big, BF), pltpu.VMEM(head.shape, BF),
            pltpu.SemaphoreType.DMA((1 + len(CUTS),)),
        ],
    )
    t1 = [moved(ta, ahead), moved(tb, ahead)]
    i1 = [moved(ia, back), moved(ib, back)]
    both_s = moved(both, swap)
    dimg, dtxt = call(home_body, [(big, F32)] * 2, both, scalars=(par,))
    t2 = [moved(t, ahead) for t in t1]
    i2 = [moved(i, back) for i in i1]
    dimg, dtxt, dimg_s, dtxt_s = call(
        near_body, [(big, F32)] * 4, *t1, *i1, both, both_s, dimg, dtxt, scalars=(par, info)
    )
    ordered, ordered2 = call(order_body, [(big, BF)] * 2, both, both_s)
    *t2, i2[0], i2[1], dimg, dtxt, dimg_s, dtxt_s, ordered, ordered2 = tie(
        (*t2, *i2, dimg, dtxt, dimg_s, dtxt_s, ordered, ordered2)
    )

    (give,) = call(
        functools.partial(give_body, 1, image_of), [(big, BF)], *t2, both_s, dimg_s,
        scalars=(par, info),
    )
    given = moved(give, swap)
    (dimg,) = call(
        functools.partial(far_body, image_of), [(big, F32)], *t2, both, dimg, scalars=(par,)
    )
    dproj, keep, send = call(
        image_end_body, [(big, BF), ((count, half), BF), ((count, half), BF)],
        dimg, given, unit_img, pnorm, scalars=(par, info),
    )
    other = moved(send, swap)
    quarter = ((half // 4, width), BF)
    parts = call(
        head_body, [quarter] * 4, keep, other, ordered, ordered2, scalars=(info,),
        scratch=[pltpu.VMEM((4, half // 4, width), BF)],
    )
    parts = list(parts)
    *i2, parts[0] = tie((*i2, parts[0]))
    parts = parts[:1] + [moved(p, ring_pairs(t, 0)) for p, t in zip(parts[1:], TURNS[1:])]
    (grad_image,) = call(grad_image_body, [(big, F32)], dproj, head)
    (give,) = call(
        functools.partial(give_body, 0, text_of), [(big, BF)], *i2, both_s, dtxt_s,
        scalars=(par, info),
    )
    (dtxt,) = call(
        functools.partial(far_body, text_of), [(big, F32)], *i2, both, dtxt, scalars=(par,)
    )
    *parts, grad_image, give, dtxt = tie((*parts, grad_image, give, dtxt))
    small = ((half // 8, half), BF)
    parts = call(
        quarter_body, [small] * 4, *parts, scalars=(info,),
        scratch=[pltpu.VMEM((4, half // 8, half), BF)],
    )
    parts = list(parts)
    given = moved(give, swap)
    parts = parts[:1] + [moved(p, ring_pairs(t, 1)) for p, t in zip(parts[1:], TURNS[1:])]
    (grad_text,) = call(text_end_body, [(big, F32)], dtxt, given, texts, scalars=(par,))
    *parts, grad_text = tie((*parts, grad_text))
    own = width // INNER
    (part,) = call(split_body, [((SIZES[3], half // 8, own), BF)], *parts)
    part = lax.all_to_all(part, "z", 0, 0)
    (part,) = call(spread_body, [((BLKS, half // 8, own), BF)], part)
    part = lax.all_to_all(part, ("yh", "x", "core"), 0, 0)
    factor = 1.0 / float(count * COUNT) ** 0.5
    (head_grad,) = call(functools.partial(join_body, factor), [((own, width), F32)], part)
    return (grad_image, grad_text, head_grad)


def solution(mesh):
    fine = Mesh(mesh.devices.reshape(SIZES), AXES)
    rows = P(AXES, None)
    return jax.shard_map(
        on_device,
        mesh=fine,
        in_specs=(rows, rows, P(), P(), P()),
        out_specs=(rows, rows, P(("z", "yl"), None)),
        check_vma=False,
    )
```

```python
import functools

import jax
import jax.numpy as jnp
import numpy as np
from jax import lax
from jax.experimental import pallas as pl
from jax.experimental.pallas import tpu as pltpu
from jax.sharding import Mesh, PartitionSpec as P

AXES = ("yh", "x", "core", "z", "yl")
SIZES = (2, 4, 2, 8, 2)
INNER = SIZES[3] * SIZES[4]
COUNT = 16 * INNER
CHIPS = SIZES[0] * SIZES[1]
BLKS = CHIPS * SIZES[2]
BF = jnp.bfloat16
F32 = jnp.float32


def chip_pairs(steps):
    shift = steps * SIZES[2] * INNER
    return [(source, (source + shift) % COUNT) for source in range(COUNT)]


def core_pairs(only=None):
    return [
        (source, source ^ INNER)
        for source in range(COUNT)
        if only is None or (source // INNER) % 2 == only
    ]


def moved(value, pairs):
    return lax.ppermute(value, AXES, pairs)


def mm(a, b, dims):
    return lax.dot_general(a, b, ((dims[:1], dims[1:]), ((), ())), preferred_element_type=F32)


def call(body, outs, *args, scalars=(), scratch=(), limit=8, space=pltpu.VMEM, small=0):
    in_specs = [pl.BlockSpec(memory_space=pltpu.SMEM)] * len(scalars)
    in_specs += [pl.BlockSpec(memory_space=space)] * len(args)
    shapes = [jax.ShapeDtypeStruct(shape, dtype) for shape, dtype in outs]
    if space is pltpu.HBM:
        args = [pltpu.with_memory_space_constraint(a, space) for a in args]
    return pl.pallas_call(
        body,
        out_shape=shapes,
        in_specs=in_specs,
        out_specs=[pl.BlockSpec(memory_space=pltpu.SMEM)] * small
        + [pl.BlockSpec(memory_space=pltpu.VMEM)] * (len(outs) - small),
        scratch_shapes=list(scratch),
        cost_estimate=pl.CostEstimate(
            flops=0,
            bytes_accessed=sum(int(np.prod(a.shape)) * a.dtype.itemsize for a in (*args, *shapes)),
            transcendentals=0,
        ),
        compiler_params=pltpu.CompilerParams(vmem_limit_bytes=limit * 2**20),
    )(*scalars, *args)


def sigmoid(x):
    return 1.0 / (1.0 + jnp.exp(-x))


def applied(par, rows, cols):
    logit = par[0] * mm(rows, cols, (1, 1)) + par[1]
    return mm(sigmoid(logit).astype(BF), cols, (1, 0))


def text_unit(texts):
    tfloat = texts.astype(F32)
    tnorm = jnp.sqrt(jnp.sum(tfloat * tfloat, -1, keepdims=True) + 1e-06)
    inverse = 1.0 / tnorm
    return tfloat * inverse, inverse


def halved(value, first, second):
    rows = value.shape[0] // 2
    first[...] = value[:rows]
    second[...] = value[rows:]


CUTS = (0, 256, 512, 768, 1152)


def start_body(
    scale, bias, images, texts, head, par,
    ta, tb, ia, ib, both, unit, norm, t_in, i_in, h_in, sems,
):
    copies = [
        pltpu.make_async_copy(texts, t_in, sems.at[0]),
        pltpu.make_async_copy(images, i_in, sems.at[1]),
    ]
    for k in range(len(CUTS) - 1):
        rows = pl.ds(CUTS[k], CUTS[k + 1] - CUTS[k])
        copies.append(pltpu.make_async_copy(head.at[rows], h_in.at[rows], sems.at[2 + k]))
    for copy in copies:
        copy.start()
    par[0] = scale[0]
    par[1] = bias[0]
    copies[0].wait()
    count = t_in.shape[0]
    low = text_unit(t_in[...])[0].astype(BF)
    halved(low, ta, tb)
    both[:count] = low
    copies[1].wait()
    both[2 * count :] = i_in[...]
    proj = None
    for k in range(len(CUTS) - 1):
        copies[2 + k].wait()
        cut = slice(CUTS[k], CUTS[k + 1])
        term = jnp.dot(i_in[:, cut], h_in[cut, :], preferred_element_type=F32)
        proj = term if proj is None else proj + term
    inverse = 1.0 / jnp.sqrt(jnp.sum(proj * proj, -1, keepdims=True) + 1e-06)
    value = proj * inverse
    unit[...] = value
    norm[...] = inverse
    low = value.astype(BF)
    halved(low, ia, ib)
    both[count : 2 * count] = low


def text_of(both):
    return both[: both.shape[0] // 3]


def image_of(both):
    count = both.shape[0] // 3
    return both[count : 2 * count]


def order_body(both, both_s, out, out2):
    own = both.shape[1] // INNER
    count = both.shape[0] // 3
    for z in range(SIZES[3]):
        for yl in range(SIZES[4]):
            source, target = (z * SIZES[4] + yl) * own, (yl * SIZES[3] + z) * own
            out[:, target : target + own] = both[2 * count :, source : source + own]
            out2[:, target : target + own] = both_s[2 * count :, source : source + own]


def home_body(par, both, dimg, dtxt):
    img_b, txt_b = image_of(both), text_of(both)
    logit = par[0] * mm(img_b, txt_b, (1, 1)) + par[1]
    eye = lax.broadcasted_iota(jnp.int32, logit.shape, 0) == lax.broadcasted_iota(
        jnp.int32, logit.shape, 1
    )
    grad = jnp.where(eye, -sigmoid(-logit), sigmoid(logit)).astype(BF)
    dimg[...] = mm(grad, txt_b, (1, 0))
    dtxt[...] = mm(grad, img_b, (0, 0))


def joined(first, second):
    return jnp.concatenate([first[...], second[...]], 0)


def near_body(par, t1a, t1b, i1a, i1b, both, both_s, dimg, dtxt, dimg_o, dtxt_o, dimg_s, dtxt_s):
    t1, i1 = joined(t1a, t1b), joined(i1a, i1b)
    dimg_o[...] = dimg[...] + applied(par, image_of(both), t1)
    dtxt_o[...] = dtxt[...] + applied(par, text_of(both), i1)
    dimg_s[...] = applied(par, image_of(both_s), t1)
    dtxt_s[...] = applied(par, text_of(both_s), i1)

    @pl.when(lax.axis_index("core") == 0)
    def _():
        dtxt_o[...] += applied(par, text_of(both), image_of(both_s))

    @pl.when(lax.axis_index("core") != 0)
    def _():
        dimg_o[...] += applied(par, image_of(both), text_of(both_s))


def give_body(giver, rows_of, par, first, second, both_s, old, out):
    @pl.when(lax.axis_index("core") == giver)
    def _():
        out[...] = (old[...] + applied(par, rows_of(both_s), joined(first, second))).astype(BF)

    @pl.when(lax.axis_index("core") != giver)
    def _():
        out[...] = old[...].astype(BF)


def far_body(rows_of, par, first, second, both, old, out):
    out[...] = old[...] + applied(par, rows_of(both), joined(first, second))


def image_end_body(par, old, given, unit, norm, whole, keep, send):
    dimg = par[0] * (old[...] + given[...].astype(F32))
    value = unit[...]
    dproj = ((dimg - value * jnp.sum(value * dimg, -1, keepdims=True)) * norm[...]).astype(BF)
    whole[...] = dproj
    half = dproj.shape[1] // 2

    @pl.when(lax.axis_index("core") == 0)
    def _():
        keep[...] = dproj[:, :half]
        send[...] = dproj[:, half:]

    @pl.when(lax.axis_index("core") != 0)
    def _():
        keep[...] = dproj[:, half:]
        send[...] = dproj[:, :half]


def text_end_body(par, old, given, texts, out):
    dtxt = par[0] * (old[...] + given[...].astype(F32))
    value, inverse = text_unit(texts[...])
    out[...] = (dtxt - value * jnp.sum(value * dtxt, -1, keepdims=True)) * inverse


TURNS = (0, 2, 1, 3)


def across_place():
    return lax.axis_index("x")


def along_place():
    return lax.axis_index("yh") * SIZES[4] + lax.axis_index("yl")


def place_of(first):
    return jnp.where(lax.axis_index("core") == first, across_place(), along_place())


def turned(place, pieces, outs):
    for turn, out in zip(TURNS, outs):
        out[...] = pieces[lax.rem(place + turn, 4)]


def head_body(keep, other, images, images2, *rest):
    outs, pieces = rest[:4], rest[4]
    total = mm(keep[...], images[...], (0, 0)) + mm(other[...], images2[...], (0, 0))
    rows, half = pieces.shape[1], total.shape[1] // 2

    @pl.when(lax.axis_index("core") == 0)
    def _():
        for k in range(4):
            pieces[k] = total[k * rows : (k + 1) * rows].astype(BF)

    @pl.when(lax.axis_index("core") != 0)
    def _():
        for k in range(4):
            up, left = 2 * (k // 2) * rows, (k % 2) * half
            first = total[up : up + rows, left : left + half]
            second = total[up + rows : up + 2 * rows, left : left + half]
            pieces[k] = jnp.concatenate([first, second], 1).astype(BF)

    turned(place_of(0), pieces, outs)


def quarter_body(a, b, c, d, *rest):
    outs, pieces = rest[:4], rest[4]
    total = a[...].astype(F32) + b[...].astype(F32) + c[...].astype(F32) + d[...].astype(F32)
    _, rows, half = pieces.shape

    def quadrant(down, right):
        return total[down * rows : (down + 1) * rows, right * half : (right + 1) * half].astype(BF)

    @pl.when(lax.axis_index("core") == 0)
    def _():
        for k in range(4):
            pieces[k] = quadrant(k // 2, k % 2)

    @pl.when(lax.axis_index("core") != 0)
    def _():
        for k in range(4):
            pieces[k] = quadrant(k % 2, k // 2)

    turned(place_of(1), pieces, outs)


def grad_image_body(dproj, head, out):
    out[...] = mm(dproj[...], head[...], (1, 1))


def split_body(a, b, c, d, out):
    total = a[...].astype(F32) + b[...].astype(F32) + c[...].astype(F32) + d[...].astype(F32)
    own = out.shape[2]
    for k in range(out.shape[0]):
        out[k] = total[:, k * own : (k + 1) * own].astype(BF)


def spread_body(parts, out):
    total = parts[0].astype(F32)
    for k in range(1, parts.shape[0]):
        total = total + parts[k].astype(F32)
    total = total.astype(BF)
    for k in range(out.shape[0]):
        out[k] = total


def join_body(factor, parts, out):
    yhs, xs, cores = SIZES[:3]
    order = [(yh * xs + x) * cores for x in range(xs) for yh in range(yhs)]
    order += [(yh * xs + x) * cores + 1 for yh in range(yhs) for x in range(xs)]
    out[...] = jnp.concatenate([parts[k].astype(F32) for k in order], 0).T * factor


def ring_pairs(turn, first):
    pairs = []
    for source in range(COUNT):
        yh, x, core, z, yl = np.unravel_index(source, SIZES)
        if core == first:
            x = (x + turn) % SIZES[1]
        else:
            y = (yh * SIZES[4] + yl + turn) % 4
            yh, yl = y // SIZES[4], y % SIZES[4]
        pairs.append((source, int(np.ravel_multi_index((yh, x, core, z, yl), SIZES))))
    return pairs


def on_device(images, texts, head, scale, bias):
    ahead, back, swap = chip_pairs(1), chip_pairs(-1), core_pairs()
    count, width = images.shape
    half = width // 2
    big = (count, width)
    tie = lax.optimization_barrier

    part_of = ((count // 2, width), BF)
    par, ta, tb, ia, ib, both, unit_img, pnorm = call(
        start_body,
        [((2,), F32)] + [part_of] * 4 + [((3 * count, width), BF), (big, F32), ((count, 1), F32)],
        images, texts, head, scalars=(scale, bias), small=1, space=pltpu.HBM, limit=16,
        scratch=[
            pltpu.VMEM(big, BF), pltpu.VMEM(big, BF), pltpu.VMEM(head.shape, BF),
            pltpu.SemaphoreType.DMA((1 + len(CUTS),)),
        ],
    )
    t1 = [moved(ta, ahead), moved(tb, ahead)]
    i1 = [moved(ia, back), moved(ib, back)]
    both_s = moved(both, swap)
    dimg, dtxt = call(home_body, [(big, F32)] * 2, both, scalars=(par,))
    t1[0], dimg, dtxt = tie((t1[0], dimg, dtxt))
    ordered, ordered2 = call(order_body, [(big, BF)] * 2, both, both_s)
    t2 = [moved(t, ahead) for t in t1]
    i2 = [moved(i, back) for i in i1]
    dimg, dtxt, dimg_s, dtxt_s = call(
        near_body, [(big, F32)] * 4, *t1, *i1, both, both_s, dimg, dtxt, scalars=(par,)
    )
    t2[0], i2[0], t2[1], dimg, dtxt, dimg_s, dtxt_s, ordered, ordered2 = tie(
        (t2[0], i2[0], t2[1], dimg, dtxt, dimg_s, dtxt_s, ordered, ordered2)
    )

    (give,) = call(
        functools.partial(give_body, 1, image_of), [(big, BF)], *t2, both_s, dimg_s,
        scalars=(par,),
    )
    i2[1], give = tie((i2[1], give))
    given = moved(give, swap)
    (dimg,) = call(
        functools.partial(far_body, image_of), [(big, F32)], *t2, both, dimg, scalars=(par,)
    )
    dproj, keep, send = call(
        image_end_body, [(big, BF), ((count, half), BF), ((count, half), BF)],
        dimg, given, unit_img, pnorm, scalars=(par,),
    )
    other = moved(send, swap)
    quarter = ((half // 4, width), BF)
    parts = call(
        head_body, [quarter] * 4, keep, other, ordered, ordered2,
        scratch=[pltpu.VMEM((4, half // 4, width), BF)],
    )
    parts = list(parts)
    parts = parts[:1] + [moved(p, ring_pairs(t, 0)) for p, t in zip(parts[1:], TURNS[1:])]
    (grad_image,) = call(grad_image_body, [(big, F32)], dproj, head)
    (give,) = call(
        functools.partial(give_body, 0, text_of), [(big, BF)], *i2, both_s, dtxt_s,
        scalars=(par,),
    )
    (dtxt,) = call(
        functools.partial(far_body, text_of), [(big, F32)], *i2, both, dtxt, scalars=(par,)
    )
    given_txt = moved(give, swap)
    *parts, grad_image, given_txt, dtxt = tie((*parts, grad_image, given_txt, dtxt))
    small = ((half // 8, half), BF)
    parts = call(
        quarter_body, [small] * 4, *parts,
        scratch=[pltpu.VMEM((4, half // 8, half), BF)],
    )
    parts = list(parts)
    parts = parts[:1] + [moved(p, ring_pairs(t, 1)) for p, t in zip(parts[1:], TURNS[1:])]
    (grad_text,) = call(text_end_body, [(big, F32)], dtxt, given_txt, texts, scalars=(par,))
    *parts, grad_text = tie((*parts, grad_text))
    own = width // INNER
    (part,) = call(split_body, [((SIZES[3], half // 8, own), BF)], *parts)
    part = lax.all_to_all(part, "z", 0, 0)
    (part,) = call(spread_body, [((BLKS, half // 8, own), BF)], part)
    part = lax.all_to_all(part, ("yh", "x", "core"), 0, 0)
    factor = 1.0 / float(count * COUNT) ** 0.5
    (head_grad,) = call(functools.partial(join_body, factor), [((own, width), F32)], part)
    return (grad_image, grad_text, head_grad)


def solution(mesh):
    fine = Mesh(mesh.devices.reshape(SIZES), AXES)
    rows = P(AXES, None)
    return jax.shard_map(
        on_device,
        mesh=fine,
        in_specs=(rows, rows, P(), P(), P()),
        out_specs=(rows, rows, P(("z", "yl"), None)),
        check_vma=False,
    )
```

```python
import functools

import jax
import jax.numpy as jnp
import numpy as np
from jax import lax
from jax.experimental import pallas as pl
from jax.experimental.pallas import tpu as pltpu
from jax.sharding import Mesh, PartitionSpec as P

AXES = ("yh", "x", "core", "z", "yl")
SIZES = (2, 4, 2, 8, 2)
INNER = SIZES[3] * SIZES[4]
COUNT = 16 * INNER
CHIPS = SIZES[0] * SIZES[1]
BLKS = CHIPS * SIZES[2]
BF = jnp.bfloat16
F32 = jnp.float32


def chip_pairs(steps):
    shift = steps * SIZES[2] * INNER
    return [(source, (source + shift) % COUNT) for source in range(COUNT)]


def mixed_pairs(kind):
    ahead, back = chip_pairs(1), chip_pairs(-1)
    return [(ahead if (k // INNER) % 2 == kind else back)[k] for k in range(COUNT)]


def core_pairs(only=None):
    return [
        (source, source ^ INNER)
        for source in range(COUNT)
        if only is None or (source // INNER) % 2 == only
    ]


def moved(value, pairs):
    return lax.ppermute(value, AXES, pairs)


def mm(a, b, dims):
    return lax.dot_general(a, b, ((dims[:1], dims[1:]), ((), ())), preferred_element_type=F32)


def call(body, outs, *args, scalars=(), scratch=(), limit=8, space=pltpu.VMEM, small=0):
    in_specs = [pl.BlockSpec(memory_space=pltpu.SMEM)] * len(scalars)
    in_specs += [pl.BlockSpec(memory_space=space)] * len(args)
    shapes = [jax.ShapeDtypeStruct(shape, dtype) for shape, dtype in outs]
    if space is pltpu.HBM:
        args = [pltpu.with_memory_space_constraint(a, space) for a in args]
    return pl.pallas_call(
        body,
        out_shape=shapes,
        in_specs=in_specs,
        out_specs=[pl.BlockSpec(memory_space=pltpu.SMEM)] * small
        + [pl.BlockSpec(memory_space=pltpu.VMEM)] * (len(outs) - small),
        scratch_shapes=list(scratch),
        cost_estimate=pl.CostEstimate(
            flops=0,
            bytes_accessed=sum(int(np.prod(a.shape)) * a.dtype.itemsize for a in (*args, *shapes)),
            transcendentals=0,
        ),
        compiler_params=pltpu.CompilerParams(vmem_limit_bytes=limit * 2**20),
    )(*scalars, *args)


def sigmoid(x):
    return 1.0 / (1.0 + jnp.exp(-x))


def logits(par, rows, cols):
    return par[0:1, 0:1] * mm(rows, cols, (1, 1)) + par[1:2, 0:1]


def applied(par, rows, cols):
    logit = logits(par, rows, cols)
    return mm(sigmoid(logit).astype(BF), cols, (1, 0))


def text_unit(texts):
    tfloat = texts.astype(F32)
    tnorm = jnp.sqrt(jnp.sum(tfloat * tfloat, -1, keepdims=True) + 1e-06)
    inverse = 1.0 / tnorm
    return tfloat * inverse, inverse


def halved(value, first, second):
    rows = value.shape[0] // 2
    first[...] = value[:rows]
    second[...] = value[rows:]


CUTS = (0, 256, 512, 768, 1152)


def start_body(
    scale, bias, images, texts, head, par,
    p1a, p1b, p2a, p2b, both, unit, norm, t_in, i_in, h_in, sems,
):
    copies = [
        pltpu.make_async_copy(texts, t_in, sems.at[0]),
        pltpu.make_async_copy(images, i_in, sems.at[1]),
    ]
    for k in range(len(CUTS) - 1):
        rows = pl.ds(CUTS[k], CUTS[k + 1] - CUTS[k])
        copies.append(pltpu.make_async_copy(head.at[rows], h_in.at[rows], sems.at[2 + k]))
    for copy in copies:
        copy.start()
    par[0:1] = jnp.full((1, par.shape[1]), scale[0], F32)
    par[1:2] = jnp.full((1, par.shape[1]), bias[0], F32)
    copies[0].wait()
    count = t_in.shape[0]
    low = text_unit(t_in[...])[0].astype(BF)
    both[:count] = low
    low_txt = low
    copies[1].wait()
    both[2 * count :] = i_in[...]
    proj = None
    for k in range(len(CUTS) - 1):
        copies[2 + k].wait()
        cut = slice(CUTS[k], CUTS[k + 1])
        term = jnp.dot(i_in[:, cut], h_in[cut, :], preferred_element_type=F32)
        proj = term if proj is None else proj + term
    inverse = 1.0 / jnp.sqrt(jnp.sum(proj * proj, -1, keepdims=True) + 1e-06)
    value = proj * inverse
    unit[...] = value
    norm[...] = inverse
    low = value.astype(BF)
    both[count : 2 * count] = low

    @pl.when(lax.axis_index("core") == 0)
    def _():
        halved(low_txt, p1a, p1b)
        halved(low, p2a, p2b)

    @pl.when(lax.axis_index("core") != 0)
    def _():
        halved(low, p1a, p1b)
        halved(low_txt, p2a, p2b)


def text_of(both):
    return both[: both.shape[0] // 3]


def image_of(both):
    count = both.shape[0] // 3
    return both[count : 2 * count]


def order_body(both, both_s, out, out2):
    own = both.shape[1] // INNER
    count = both.shape[0] // 3
    for z in range(SIZES[3]):
        for yl in range(SIZES[4]):
            source, target = (z * SIZES[4] + yl) * own, (yl * SIZES[3] + z) * own
            out[:, target : target + own] = both[2 * count :, source : source + own]
            out2[:, target : target + own] = both_s[2 * count :, source : source + own]


def home_body(par, both, dimg, dtxt):
    img_b, txt_b = image_of(both), text_of(both)
    logit = logits(par, img_b, txt_b)
    eye = lax.broadcasted_iota(jnp.int32, logit.shape, 0) == lax.broadcasted_iota(
        jnp.int32, logit.shape, 1
    )
    grad = jnp.where(eye, -sigmoid(-logit), sigmoid(logit)).astype(BF)
    dimg[...] = mm(grad, txt_b, (1, 0))
    dtxt[...] = mm(grad, img_b, (0, 0))


def joined(one, two, kind):
    here = lax.axis_index("core") == kind
    return jnp.concatenate([jnp.where(here, a[...], b[...]) for a, b in zip(one, two)], 0)


def near_body(par, p1a, p1b, p2a, p2b, both, both_s, dimg, dtxt, dimg_o, dtxt_o, dimg_s, dtxt_s):
    t1, i1 = (joined((p1a, p1b), (p2a, p2b), kind) for kind in range(2))
    dimg_o[...] = dimg[...] + applied(par, image_of(both), t1)
    dtxt_o[...] = dtxt[...] + applied(par, text_of(both), i1)
    dimg_s[...] = applied(par, image_of(both_s), t1)
    dtxt_s[...] = applied(par, text_of(both_s), i1)

    @pl.when(lax.axis_index("core") == 0)
    def _():
        dtxt_o[...] += applied(par, text_of(both), image_of(both_s))

    @pl.when(lax.axis_index("core") != 0)
    def _():
        dimg_o[...] += applied(par, image_of(both), text_of(both_s))


def give_body(giver, kind, rows_of, par, p1a, p1b, p2a, p2b, both_s, old, out):
    @pl.when(lax.axis_index("core") == giver)
    def _():
        out[...] = (old[...] + applied(par, rows_of(both_s), joined((p1a, p1b), (p2a, p2b), kind))).astype(BF)

    @pl.when(lax.axis_index("core") != giver)
    def _():
        out[...] = old[...].astype(BF)


def far_body(kind, rows_of, par, p1a, p1b, p2a, p2b, both, old, out):
    out[...] = old[...] + applied(par, rows_of(both), joined((p1a, p1b), (p2a, p2b), kind))


def image_end_body(par, old, given, unit, norm, whole, keep, send):
    dimg = par[0:1, 0:1] * (old[...] + given[...].astype(F32))
    value = unit[...]
    dproj = ((dimg - value * jnp.sum(value * dimg, -1, keepdims=True)) * norm[...]).astype(BF)
    whole[...] = dproj
    half = dproj.shape[1] // 2

    @pl.when(lax.axis_index("core") == 0)
    def _():
        keep[...] = dproj[:, :half]
        send[...] = dproj[:, half:]

    @pl.when(lax.axis_index("core") != 0)
    def _():
        keep[...] = dproj[:, half:]
        send[...] = dproj[:, :half]


def text_end_body(par, old, given, texts, out):
    dtxt = par[0:1, 0:1] * (old[...] + given[...].astype(F32))
    value, inverse = text_unit(texts[...])
    out[...] = (dtxt - value * jnp.sum(value * dtxt, -1, keepdims=True)) * inverse


TURNS = (0, 2, 1, 3)


def across_place():
    return lax.axis_index("x")


def along_place():
    return lax.axis_index("yh") * SIZES[4] + lax.axis_index("yl")


def place_of(first):
    return jnp.where(lax.axis_index("core") == first, across_place(), along_place())


def turned(place, pieces, outs):
    for turn, out in zip(TURNS, outs):
        out[...] = pieces[lax.rem(place + turn, 4)]


def head_body(keep, other, images, images2, *rest):
    outs, pieces = rest[:4], rest[4]
    total = mm(keep[...], images[...], (0, 0)) + mm(other[...], images2[...], (0, 0))
    rows, half = pieces.shape[1], total.shape[1] // 2

    @pl.when(lax.axis_index("core") == 0)
    def _():
        for k in range(4):
            pieces[k] = total[k * rows : (k + 1) * rows].astype(BF)

    @pl.when(lax.axis_index("core") != 0)
    def _():
        for k in range(4):
            up, left = 2 * (k // 2) * rows, (k % 2) * half
            first = total[up : up + rows, left : left + half]
            second = total[up + rows : up + 2 * rows, left : left + half]
            pieces[k] = jnp.concatenate([first, second], 1).astype(BF)

    turned(place_of(0), pieces, outs)


def quarter_body(a, b, c, d, *rest):
    outs, pieces = rest[:4], rest[4]
    total = a[...].astype(F32) + b[...].astype(F32) + c[...].astype(F32) + d[...].astype(F32)
    _, rows, half = pieces.shape

    def quadrant(down, right):
        return total[down * rows : (down + 1) * rows, right * half : (right + 1) * half].astype(BF)

    @pl.when(lax.axis_index("core") == 0)
    def _():
        for k in range(4):
            pieces[k] = quadrant(k // 2, k % 2)

    @pl.when(lax.axis_index("core") != 0)
    def _():
        for k in range(4):
            pieces[k] = quadrant(k % 2, k // 2)

    turned(place_of(1), pieces, outs)


def grad_image_body(dproj, head, out):
    out[...] = mm(dproj[...], head[...], (1, 1))


def split_body(a, b, c, d, out):
    total = a[...].astype(F32) + b[...].astype(F32) + c[...].astype(F32) + d[...].astype(F32)
    own = out.shape[2]
    for k in range(out.shape[0]):
        out[k] = total[:, k * own : (k + 1) * own].astype(BF)


def spread_body(parts, out):
    total = parts[0].astype(F32)
    for k in range(1, parts.shape[0]):
        total = total + parts[k].astype(F32)
    total = total.astype(BF)
    for k in range(out.shape[0]):
        out[k] = total


def join_body(factor, parts, out):
    yhs, xs, cores = SIZES[:3]
    order = [(yh * xs + x) * cores for x in range(xs) for yh in range(yhs)]
    order += [(yh * xs + x) * cores + 1 for yh in range(yhs) for x in range(xs)]
    out[...] = jnp.concatenate([parts[k].astype(F32) for k in order], 0).T * factor


def ring_pairs(turn, first):
    pairs = []
    for source in range(COUNT):
        yh, x, core, z, yl = np.unravel_index(source, SIZES)
        if core == first:
            x = (x + turn) % SIZES[1]
        else:
            y = (yh * SIZES[4] + yl + turn) % 4
            yh, yl = y // SIZES[4], y % SIZES[4]
        pairs.append((source, int(np.ravel_multi_index((yh, x, core, z, yl), SIZES))))
    return pairs


def on_device(images, texts, head, scale, bias):
    swap = core_pairs()
    count, width = images.shape
    half = width // 2
    big = (count, width)
    tie = lax.optimization_barrier

    part_of = ((count // 2, width), BF)
    par, p1a, p1b, p2a, p2b, both, unit_img, pnorm = call(
        start_body,
        [((2, 128), F32)] + [part_of] * 4 + [((3 * count, width), BF), (big, F32), ((count, 1), F32)],
        images, texts, head, scalars=(scale, bias), space=pltpu.HBM, limit=16,
        scratch=[
            pltpu.VMEM(big, BF), pltpu.VMEM(big, BF), pltpu.VMEM(head.shape, BF),
            pltpu.SemaphoreType.DMA((1 + len(CUTS),)),
        ],
    )
    ways = (mixed_pairs(0), mixed_pairs(1))
    near = [moved(p1a, ways[0]), moved(p2a, ways[1]), moved(p1b, ways[0]), moved(p2b, ways[1])]
    both_s = moved(both, swap)
    dimg, dtxt = call(home_body, [(big, F32)] * 2, par, both)
    near[0], dimg, dtxt = tie((near[0], dimg, dtxt))
    ordered, ordered2 = call(order_body, [(big, BF)] * 2, both, both_s)
    far = [moved(p, ways[k % 2]) for k, p in enumerate(near)]
    dimg, dtxt, dimg_s, dtxt_s = call(
        near_body, [(big, F32)] * 4, par, near[0], near[2], near[1], near[3], both, both_s, dimg, dtxt
    )
    *far, dimg, dtxt, dimg_s, dtxt_s, ordered, ordered2 = tie(
        (*far, dimg, dtxt, dimg_s, dtxt_s, ordered, ordered2)
    )
    far = [far[0], far[2], far[1], far[3]]

    (give,) = call(
        functools.partial(give_body, 1, 0, image_of), [(big, BF)], par, *far, both_s, dimg_s
    )
    given = moved(give, swap)
    (dimg,) = call(
        functools.partial(far_body, 0, image_of), [(big, F32)], par, *far, both, dimg
    )
    dproj, keep, send = call(
        image_end_body, [(big, BF), ((count, half), BF), ((count, half), BF)],
        par, dimg, given, unit_img, pnorm,
    )
    other = moved(send, swap)
    quarter = ((half // 4, width), BF)
    parts = call(
        head_body, [quarter] * 4, keep, other, ordered, ordered2,
        scratch=[pltpu.VMEM((4, half // 4, width), BF)],
    )
    parts = list(parts)
    parts = parts[:1] + [moved(p, ring_pairs(t, 0)) for p, t in zip(parts[1:], TURNS[1:])]
    (grad_image,) = call(grad_image_body, [(big, F32)], dproj, head)
    (give,) = call(
        functools.partial(give_body, 0, 1, text_of), [(big, BF)], par, *far, both_s, dtxt_s
    )
    (dtxt,) = call(
        functools.partial(far_body, 1, text_of), [(big, F32)], par, *far, both, dtxt
    )
    given_txt = moved(give, swap)
    *parts, grad_image, given_txt, dtxt = tie((*parts, grad_image, given_txt, dtxt))
    small = ((half // 8, half), BF)
    parts = call(
        quarter_body, [small] * 4, *parts,
        scratch=[pltpu.VMEM((4, half // 8, half), BF)],
    )
    parts = list(parts)
    parts = parts[:1] + [moved(p, ring_pairs(t, 1)) for p, t in zip(parts[1:], TURNS[1:])]
    (grad_text,) = call(text_end_body, [(big, F32)], par, dtxt, given_txt, texts)
    *parts, grad_text = tie((*parts, grad_text))
    own = width // INNER
    (part,) = call(split_body, [((SIZES[3], half // 8, own), BF)], *parts)
    part = lax.all_to_all(part, "z", 0, 0)
    (part,) = call(spread_body, [((BLKS, half // 8, own), BF)], part)
    part = lax.all_to_all(part, ("yh", "x", "core"), 0, 0)
    factor = 1.0 / float(count * COUNT) ** 0.5
    (head_grad,) = call(functools.partial(join_body, factor), [((own, width), F32)], part)
    return (grad_image, grad_text, head_grad)


def solution(mesh):
    fine = Mesh(mesh.devices.reshape(SIZES), AXES)
    rows = P(AXES, None)
    return jax.shard_map(
        on_device,
        mesh=fine,
        in_specs=(rows, rows, P(), P(), P()),
        out_specs=(rows, rows, P(("z", "yl"), None)),
        check_vma=False,
    )
```

```python
import functools

import jax
import jax.numpy as jnp
import numpy as np
from jax import lax
from jax.experimental import pallas as pl
from jax.experimental.pallas import tpu as pltpu
from jax.sharding import Mesh, PartitionSpec as P

AXES = ("yh", "x", "core", "z", "yl")
SIZES = (2, 4, 2, 8, 2)
INNER = SIZES[3] * SIZES[4]
COUNT = 16 * INNER
CHIPS = SIZES[0] * SIZES[1]
BLKS = CHIPS * SIZES[2]
BF = jnp.bfloat16
F32 = jnp.float32


def chip_pairs(steps):
    shift = steps * SIZES[2] * INNER
    return [(source, (source + shift) % COUNT) for source in range(COUNT)]


def mixed_pairs(kind):
    ahead, back = chip_pairs(1), chip_pairs(-1)
    return [(ahead if (k // INNER) % 2 == kind else back)[k] for k in range(COUNT)]


def core_pairs(only=None):
    return [
        (source, source ^ INNER)
        for source in range(COUNT)
        if only is None or (source // INNER) % 2 == only
    ]


def moved(value, pairs):
    return lax.ppermute(value, AXES, pairs)


def mm(a, b, dims):
    return lax.dot_general(a, b, ((dims[:1], dims[1:]), ((), ())), preferred_element_type=F32)


def call(body, outs, *args, scalars=(), scratch=(), limit=8, space=pltpu.VMEM, small=0):
    in_specs = [pl.BlockSpec(memory_space=pltpu.SMEM)] * len(scalars)
    in_specs += [pl.BlockSpec(memory_space=space)] * len(args)
    shapes = [jax.ShapeDtypeStruct(shape, dtype) for shape, dtype in outs]
    if space is pltpu.HBM:
        args = [pltpu.with_memory_space_constraint(a, space) for a in args]
    return pl.pallas_call(
        body,
        out_shape=shapes,
        in_specs=in_specs,
        out_specs=[pl.BlockSpec(memory_space=pltpu.SMEM)] * small
        + [pl.BlockSpec(memory_space=pltpu.VMEM)] * (len(outs) - small),
        scratch_shapes=list(scratch),
        cost_estimate=pl.CostEstimate(
            flops=0,
            bytes_accessed=sum(int(np.prod(a.shape)) * a.dtype.itemsize for a in (*args, *shapes)),
            transcendentals=0,
        ),
        compiler_params=pltpu.CompilerParams(vmem_limit_bytes=limit * 2**20),
    )(*scalars, *args)


def sigmoid(x):
    return 1.0 / (1.0 + jnp.exp(-x))


def logits(par, rows, cols):
    return par[0:1, 0:1] * mm(rows, cols, (1, 1)) + par[1:2, 0:1]


def applied(par, rows, cols):
    logit = logits(par, rows, cols)
    return mm(sigmoid(logit).astype(BF), cols, (1, 0))


def text_unit(texts):
    tfloat = texts.astype(F32)
    tnorm = jnp.sqrt(jnp.sum(tfloat * tfloat, -1, keepdims=True) + 1e-06)
    inverse = 1.0 / tnorm
    return tfloat * inverse, inverse


def halved(value, first, second):
    rows = value.shape[0] // 2
    first[...] = value[:rows]
    second[...] = value[rows:]


CUTS = (0, 256, 512, 768, 1152)


def start_body(
    scale, bias, images, texts, head, par,
    p1a, p1b, p2a, p2b, both, unit, norm, t_in, i_in, h_in, sems,
):
    copies = [
        pltpu.make_async_copy(texts, t_in, sems.at[0]),
        pltpu.make_async_copy(images, i_in, sems.at[1]),
    ]
    for k in range(len(CUTS) - 1):
        rows = pl.ds(CUTS[k], CUTS[k + 1] - CUTS[k])
        copies.append(pltpu.make_async_copy(head.at[rows], h_in.at[rows], sems.at[2 + k]))
    for copy in copies:
        copy.start()
    par[0:1] = jnp.full((1, par.shape[1]), scale[0], F32)
    par[1:2] = jnp.full((1, par.shape[1]), bias[0], F32)
    copies[0].wait()
    count = t_in.shape[0]
    low = text_unit(t_in[...])[0].astype(BF)
    both[:count] = low
    low_txt = low
    copies[1].wait()
    both[2 * count :] = i_in[...]
    proj = None
    for k in range(len(CUTS) - 1):
        copies[2 + k].wait()
        cut = slice(CUTS[k], CUTS[k + 1])
        term = jnp.dot(i_in[:, cut], h_in[cut, :], preferred_element_type=F32)
        proj = term if proj is None else proj + term
    inverse = 1.0 / jnp.sqrt(jnp.sum(proj * proj, -1, keepdims=True) + 1e-06)
    value = proj * inverse
    unit[...] = value
    norm[...] = inverse
    low = value.astype(BF)
    both[count : 2 * count] = low

    @pl.when(lax.axis_index("core") == 0)
    def _():
        halved(low_txt, p1a, p1b)
        halved(low, p2a, p2b)

    @pl.when(lax.axis_index("core") != 0)
    def _():
        halved(low, p1a, p1b)
        halved(low_txt, p2a, p2b)


def text_of(both):
    return both[: both.shape[0] // 3]


def image_of(both):
    count = both.shape[0] // 3
    return both[count : 2 * count]


def order_body(both, both_s, out, out2):
    own = both.shape[1] // INNER
    count = both.shape[0] // 3
    for z in range(SIZES[3]):
        for yl in range(SIZES[4]):
            source, target = (z * SIZES[4] + yl) * own, (yl * SIZES[3] + z) * own
            out[:, target : target + own] = both[2 * count :, source : source + own]
            out2[:, target : target + own] = both_s[2 * count :, source : source + own]


def home_body(par, both, dimg, dtxt):
    img_b, txt_b = image_of(both), text_of(both)
    logit = logits(par, img_b, txt_b)
    eye = lax.broadcasted_iota(jnp.int32, logit.shape, 0) == lax.broadcasted_iota(
        jnp.int32, logit.shape, 1
    )
    grad = jnp.where(eye, -sigmoid(-logit), sigmoid(logit)).astype(BF)
    dimg[...] = mm(grad, txt_b, (1, 0))
    dtxt[...] = mm(grad, img_b, (0, 0))


def joined(one, two, kind):
    here = lax.axis_index("core") == kind
    return jnp.concatenate([jnp.where(here, a[...], b[...]) for a, b in zip(one, two)], 0)


def near_body(par, p1a, p1b, p2a, p2b, both, both_s, dimg, dtxt, dimg_o, dtxt_o, dimg_s, dtxt_s):
    t1, i1 = (joined((p1a, p1b), (p2a, p2b), kind) for kind in range(2))
    dimg_o[...] = dimg[...] + applied(par, image_of(both), t1)
    dtxt_o[...] = dtxt[...] + applied(par, text_of(both), i1)
    dimg_s[...] = applied(par, image_of(both_s), t1)
    dtxt_s[...] = applied(par, text_of(both_s), i1)

    @pl.when(lax.axis_index("core") == 0)
    def _():
        dtxt_o[...] += applied(par, text_of(both), image_of(both_s))

    @pl.when(lax.axis_index("core") != 0)
    def _():
        dimg_o[...] += applied(par, image_of(both), text_of(both_s))


def give_body(giver, kind, rows_of, par, p1a, p1b, p2a, p2b, both_s, old, out):
    @pl.when(lax.axis_index("core") == giver)
    def _():
        out[...] = (old[...] + applied(par, rows_of(both_s), joined((p1a, p1b), (p2a, p2b), kind))).astype(BF)

    @pl.when(lax.axis_index("core") != giver)
    def _():
        out[...] = old[...].astype(BF)


def far_body(kind, rows_of, par, p1a, p1b, p2a, p2b, both, old, out):
    out[...] = old[...] + applied(par, rows_of(both), joined((p1a, p1b), (p2a, p2b), kind))


def image_end_body(par, old, given, unit, norm, whole, keep, send):
    dimg = par[0:1, 0:1] * (old[...] + given[...].astype(F32))
    value = unit[...]
    dproj = ((dimg - value * jnp.sum(value * dimg, -1, keepdims=True)) * norm[...]).astype(BF)
    whole[...] = dproj
    half = dproj.shape[1] // 2

    @pl.when(lax.axis_index("core") == 0)
    def _():
        keep[...] = dproj[:, :half]
        send[...] = dproj[:, half:]

    @pl.when(lax.axis_index("core") != 0)
    def _():
        keep[...] = dproj[:, half:]
        send[...] = dproj[:, :half]


def text_end_body(par, old, given, texts, out):
    dtxt = par[0:1, 0:1] * (old[...] + given[...].astype(F32))
    value, inverse = text_unit(texts[...])
    out[...] = (dtxt - value * jnp.sum(value * dtxt, -1, keepdims=True)) * inverse


TURNS = (0, 2, 1, 3)


def across_place():
    return lax.axis_index("x")


def along_place():
    return lax.axis_index("yh") * SIZES[4] + lax.axis_index("yl")


def place_of(first):
    return jnp.where(lax.axis_index("core") == first, across_place(), along_place())


def turned(place, pieces, outs):
    for turn, out in zip(TURNS, outs):
        out[...] = pieces[lax.rem(place + turn, 4)]


def head_body(keep, other, images, images2, *rest):
    outs, pieces = rest[:4], rest[4]
    total = mm(keep[...], images[...], (0, 0)) + mm(other[...], images2[...], (0, 0))
    rows, half = pieces.shape[1], total.shape[1] // 2

    @pl.when(lax.axis_index("core") == 0)
    def _():
        for k in range(4):
            pieces[k] = total[k * rows : (k + 1) * rows].astype(BF)

    @pl.when(lax.axis_index("core") != 0)
    def _():
        for k in range(4):
            up, left = 2 * (k // 2) * rows, (k % 2) * half
            first = total[up : up + rows, left : left + half]
            second = total[up + rows : up + 2 * rows, left : left + half]
            pieces[k] = jnp.concatenate([first, second], 1).astype(BF)

    turned(place_of(0), pieces, outs)


def quarter_body(a, b, c, d, *rest):
    outs, pieces = rest[:4], rest[4]
    total = a[...].astype(F32) + b[...].astype(F32) + c[...].astype(F32) + d[...].astype(F32)
    _, rows, half = pieces.shape

    def quadrant(down, right):
        return total[down * rows : (down + 1) * rows, right * half : (right + 1) * half].astype(BF)

    @pl.when(lax.axis_index("core") == 0)
    def _():
        for k in range(4):
            pieces[k] = quadrant(k // 2, k % 2)

    @pl.when(lax.axis_index("core") != 0)
    def _():
        for k in range(4):
            pieces[k] = quadrant(k % 2, k // 2)

    turned(place_of(1), pieces, outs)


def grad_image_body(dproj, head, out):
    out[...] = mm(dproj[...], head[...], (1, 1))


FOLD = 3


def folded(piece):
    rows = piece.shape[0] // FOLD
    return jnp.concatenate([piece[k * rows : (k + 1) * rows] for k in range(FOLD)], 1)


def unfolded(piece):
    width = piece.shape[1] // FOLD
    return jnp.concatenate([piece[:, k * width : (k + 1) * width] for k in range(FOLD)], 0)


def split_body(a, b, c, d, out):
    total = a[...].astype(F32) + b[...].astype(F32) + c[...].astype(F32) + d[...].astype(F32)
    own = out.shape[2] // FOLD
    for k in range(out.shape[0]):
        out[k] = folded(total[:, k * own : (k + 1) * own]).astype(BF)


def spread_body(parts, out):
    total = parts[0].astype(F32)
    for k in range(1, parts.shape[0]):
        total = total + parts[k].astype(F32)
    total = total.astype(BF)
    for k in range(out.shape[0]):
        out[k] = total


def join_body(factor, parts, out):
    yhs, xs, cores = SIZES[:3]
    order = [(yh * xs + x) * cores for x in range(xs) for yh in range(yhs)]
    order += [(yh * xs + x) * cores + 1 for yh in range(yhs) for x in range(xs)]
    out[...] = jnp.concatenate([unfolded(parts[k].astype(F32)) for k in order], 0).T * factor


def ring_pairs(turn, first):
    pairs = []
    for source in range(COUNT):
        yh, x, core, z, yl = np.unravel_index(source, SIZES)
        if core == first:
            x = (x + turn) % SIZES[1]
        else:
            y = (yh * SIZES[4] + yl + turn) % 4
            yh, yl = y // SIZES[4], y % SIZES[4]
        pairs.append((source, int(np.ravel_multi_index((yh, x, core, z, yl), SIZES))))
    return pairs


def on_device(images, texts, head, scale, bias):
    swap = core_pairs()
    count, width = images.shape
    half = width // 2
    big = (count, width)
    tie = lax.optimization_barrier

    part_of = ((count // 2, width), BF)
    par, p1a, p1b, p2a, p2b, both, unit_img, pnorm = call(
        start_body,
        [((2, 128), F32)] + [part_of] * 4 + [((3 * count, width), BF), (big, F32), ((count, 1), F32)],
        images, texts, head, scalars=(scale, bias), space=pltpu.HBM, limit=16,
        scratch=[
            pltpu.VMEM(big, BF), pltpu.VMEM(big, BF), pltpu.VMEM(head.shape, BF),
            pltpu.SemaphoreType.DMA((1 + len(CUTS),)),
        ],
    )
    ways = (mixed_pairs(0), mixed_pairs(1))
    near = [moved(p1a, ways[0]), moved(p2a, ways[1]), moved(p1b, ways[0]), moved(p2b, ways[1])]
    both_s = moved(both, swap)
    dimg, dtxt = call(home_body, [(big, F32)] * 2, par, both)
    near[0], dimg, dtxt = tie((near[0], dimg, dtxt))
    ordered, ordered2 = call(order_body, [(big, BF)] * 2, both, both_s)
    far = [moved(p, ways[k % 2]) for k, p in enumerate(near)]
    dimg, dtxt, dimg_s, dtxt_s = call(
        near_body, [(big, F32)] * 4, par, near[0], near[2], near[1], near[3], both, both_s, dimg, dtxt
    )
    *far, dimg, dtxt, dimg_s, dtxt_s, ordered, ordered2 = tie(
        (*far, dimg, dtxt, dimg_s, dtxt_s, ordered, ordered2)
    )
    far = [far[0], far[2], far[1], far[3]]

    (give,) = call(
        functools.partial(give_body, 1, 0, image_of), [(big, BF)], par, *far, both_s, dimg_s
    )
    given = moved(give, swap)
    (dimg,) = call(
        functools.partial(far_body, 0, image_of), [(big, F32)], par, *far, both, dimg
    )
    dproj, keep, send = call(
        image_end_body, [(big, BF), ((count, half), BF), ((count, half), BF)],
        par, dimg, given, unit_img, pnorm,
    )
    other = moved(send, swap)
    quarter = ((half // 4, width), BF)
    parts = call(
        head_body, [quarter] * 4, keep, other, ordered, ordered2,
        scratch=[pltpu.VMEM((4, half // 4, width), BF)],
    )
    parts = list(parts)
    parts = parts[:1] + [moved(p, ring_pairs(t, 0)) for p, t in zip(parts[1:], TURNS[1:])]
    (grad_image,) = call(grad_image_body, [(big, F32)], dproj, head)
    (give,) = call(
        functools.partial(give_body, 0, 1, text_of), [(big, BF)], par, *far, both_s, dtxt_s
    )
    (dtxt,) = call(
        functools.partial(far_body, 1, text_of), [(big, F32)], par, *far, both, dtxt
    )
    given_txt = moved(give, swap)
    *parts, grad_image, given_txt, dtxt = tie((*parts, grad_image, given_txt, dtxt))
    small = ((half // 8, half), BF)
    parts = call(
        quarter_body, [small] * 4, *parts,
        scratch=[pltpu.VMEM((4, half // 8, half), BF)],
    )
    parts = list(parts)
    parts = parts[:1] + [moved(p, ring_pairs(t, 1)) for p, t in zip(parts[1:], TURNS[1:])]
    (grad_text,) = call(text_end_body, [(big, F32)], par, dtxt, given_txt, texts)
    *parts, grad_text = tie((*parts, grad_text))
    own = width // INNER
    (part,) = call(split_body, [((SIZES[3], half // 8 // FOLD, own * FOLD), BF)], *parts)
    part = lax.all_to_all(part, "z", 0, 0)
    (part,) = call(spread_body, [((BLKS, half // 8 // FOLD, own * FOLD), BF)], part)
    part = lax.all_to_all(part, ("yh", "x", "core"), 0, 0)
    factor = 1.0 / float(count * COUNT) ** 0.5
    (head_grad,) = call(functools.partial(join_body, factor), [((own, width), F32)], part)
    return (grad_image, grad_text, head_grad)


def solution(mesh):
    fine = Mesh(mesh.devices.reshape(SIZES), AXES)
    rows = P(AXES, None)
    return jax.shard_map(
        on_device,
        mesh=fine,
        in_specs=(rows, rows, P(), P(), P()),
        out_specs=(rows, rows, P(("z", "yl"), None)),
        check_vma=False,
    )
```

```python
import functools

import jax
import jax.numpy as jnp
import numpy as np
from jax import lax
from jax.experimental import pallas as pl
from jax.experimental.pallas import tpu as pltpu
from jax.sharding import Mesh, PartitionSpec as P

AXES = ("yh", "x", "core", "z", "yl")
SIZES = (2, 4, 2, 8, 2)
INNER = SIZES[3] * SIZES[4]
COUNT = 16 * INNER
CHIPS = SIZES[0] * SIZES[1]
BLKS = CHIPS * SIZES[2]
BF = jnp.bfloat16
F32 = jnp.float32


def chip_pairs(steps):
    shift = steps * SIZES[2] * INNER
    return [(source, (source + shift) % COUNT) for source in range(COUNT)]


def mixed_pairs(kind):
    ahead, back = chip_pairs(1), chip_pairs(-1)
    return [(ahead if (k // INNER) % 2 == kind else back)[k] for k in range(COUNT)]


def core_pairs(only=None):
    return [
        (source, source ^ INNER)
        for source in range(COUNT)
        if only is None or (source // INNER) % 2 == only
    ]


def moved(value, pairs):
    return lax.ppermute(value, AXES, pairs)


def mm(a, b, dims):
    return lax.dot_general(a, b, ((dims[:1], dims[1:]), ((), ())), preferred_element_type=F32)


def call(body, outs, *args, scalars=(), scratch=(), limit=8, space=pltpu.VMEM, small=0):
    in_specs = [pl.BlockSpec(memory_space=pltpu.SMEM)] * len(scalars)
    in_specs += [pl.BlockSpec(memory_space=space)] * len(args)
    shapes = [jax.ShapeDtypeStruct(shape, dtype) for shape, dtype in outs]
    if space is pltpu.HBM:
        args = [pltpu.with_memory_space_constraint(a, space) for a in args]
    return pl.pallas_call(
        body,
        out_shape=shapes,
        in_specs=in_specs,
        out_specs=[pl.BlockSpec(memory_space=pltpu.SMEM)] * small
        + [pl.BlockSpec(memory_space=pltpu.VMEM)] * (len(outs) - small),
        scratch_shapes=list(scratch),
        cost_estimate=pl.CostEstimate(
            flops=0,
            bytes_accessed=sum(int(np.prod(a.shape)) * a.dtype.itemsize for a in (*args, *shapes)),
            transcendentals=0,
        ),
        compiler_params=pltpu.CompilerParams(vmem_limit_bytes=limit * 2**20),
    )(*scalars, *args)


def sigmoid(x):
    return 1.0 / (1.0 + jnp.exp(-x))


def logits(par, rows, cols):
    return par[0:1, 0:1] * mm(rows, cols, (1, 1)) + par[1:2, 0:1]


def applied(par, rows, cols):
    logit = logits(par, rows, cols)
    return mm(sigmoid(logit).astype(BF), cols, (1, 0))


def text_unit(texts):
    tfloat = texts.astype(F32)
    tnorm = jnp.sqrt(jnp.sum(tfloat * tfloat, -1, keepdims=True) + 1e-06)
    inverse = 1.0 / tnorm
    return tfloat * inverse, inverse


def halved(value, first, second):
    rows = value.shape[0] // 2
    first[...] = value[:rows]
    second[...] = value[rows:]


CUTS = (0, 256, 512, 768, 1152)


def start_body(
    scale, bias, images, texts, head, par,
    p1a, p1b, p2a, p2b, both, unit, norm, t_in, i_in, h_in, sems,
):
    copies = [
        pltpu.make_async_copy(texts, t_in, sems.at[0]),
        pltpu.make_async_copy(images, i_in, sems.at[1]),
    ]
    for k in range(len(CUTS) - 1):
        rows = pl.ds(CUTS[k], CUTS[k + 1] - CUTS[k])
        copies.append(pltpu.make_async_copy(head.at[rows], h_in.at[rows], sems.at[2 + k]))
    for copy in copies:
        copy.start()
    par[0:1] = jnp.full((1, par.shape[1]), scale[0], F32)
    par[1:2] = jnp.full((1, par.shape[1]), bias[0], F32)
    copies[0].wait()
    count = t_in.shape[0]
    low = text_unit(t_in[...])[0].astype(BF)
    both[:count] = low
    low_txt = low
    copies[1].wait()
    both[2 * count :] = i_in[...]
    proj = None
    for k in range(len(CUTS) - 1):
        copies[2 + k].wait()
        cut = slice(CUTS[k], CUTS[k + 1])
        term = jnp.dot(i_in[:, cut], h_in[cut, :], preferred_element_type=F32)
        proj = term if proj is None else proj + term
    inverse = 1.0 / jnp.sqrt(jnp.sum(proj * proj, -1, keepdims=True) + 1e-06)
    value = proj * inverse
    unit[...] = value
    norm[...] = inverse
    low = value.astype(BF)
    both[count : 2 * count] = low

    @pl.when(lax.axis_index("core") == 0)
    def _():
        halved(low_txt, p1a, p1b)
        halved(low, p2a, p2b)

    @pl.when(lax.axis_index("core") != 0)
    def _():
        halved(low, p1a, p1b)
        halved(low_txt, p2a, p2b)


def text_of(both):
    return both[: both.shape[0] // 3]


def image_of(both):
    count = both.shape[0] // 3
    return both[count : 2 * count]


def order_body(both, both_s, out, out2):
    own = both.shape[1] // INNER
    count = both.shape[0] // 3
    for z in range(SIZES[3]):
        for yl in range(SIZES[4]):
            source, target = (z * SIZES[4] + yl) * own, (yl * SIZES[3] + z) * own
            out[:, target : target + own] = both[2 * count :, source : source + own]
            out2[:, target : target + own] = both_s[2 * count :, source : source + own]


def home_body(par, both, dimg, dtxt):
    img_b, txt_b = image_of(both), text_of(both)
    logit = logits(par, img_b, txt_b)
    eye = lax.broadcasted_iota(jnp.int32, logit.shape, 0) == lax.broadcasted_iota(
        jnp.int32, logit.shape, 1
    )
    grad = jnp.where(eye, -sigmoid(-logit), sigmoid(logit)).astype(BF)
    dimg[...] = mm(grad, txt_b, (1, 0))
    dtxt[...] = mm(grad, img_b, (0, 0))


def half_of(one, two, kind):
    return jnp.where(lax.axis_index("core") == kind, one[...], two[...])


def give_first_body(par, one, two, both_s, old, out):
    out[...] = old[...]

    @pl.when(lax.axis_index("core") == 1)
    def _():
        out[...] += applied(par, image_of(both_s), half_of(one, two, 0))


def give_last_body(par, one, two, both_s, old, out):
    @pl.when(lax.axis_index("core") == 1)
    def _():
        out[...] = (old[...] + applied(par, image_of(both_s), half_of(one, two, 0))).astype(BF)

    @pl.when(lax.axis_index("core") != 1)
    def _():
        out[...] = old[...].astype(BF)


def far_half_body(par, one, two, both, old, out):
    out[...] = old[...] + applied(par, image_of(both), half_of(one, two, 0))


def joined(one, two, kind):
    here = lax.axis_index("core") == kind
    return jnp.concatenate([jnp.where(here, a[...], b[...]) for a, b in zip(one, two)], 0)


def near_body(par, p1a, p1b, p2a, p2b, both, both_s, dimg, dtxt, dimg_o, dtxt_o, dimg_s, dtxt_s):
    t1, i1 = (joined((p1a, p1b), (p2a, p2b), kind) for kind in range(2))
    dimg_o[...] = dimg[...] + applied(par, image_of(both), t1)
    dtxt_o[...] = dtxt[...] + applied(par, text_of(both), i1)
    dimg_s[...] = applied(par, image_of(both_s), t1)
    dtxt_s[...] = applied(par, text_of(both_s), i1)

    @pl.when(lax.axis_index("core") == 0)
    def _():
        dtxt_o[...] += applied(par, text_of(both), image_of(both_s))

    @pl.when(lax.axis_index("core") != 0)
    def _():
        dimg_o[...] += applied(par, image_of(both), text_of(both_s))


def give_body(giver, kind, rows_of, par, p1a, p1b, p2a, p2b, both_s, old, out):
    @pl.when(lax.axis_index("core") == giver)
    def _():
        out[...] = (old[...] + applied(par, rows_of(both_s), joined((p1a, p1b), (p2a, p2b), kind))).astype(BF)

    @pl.when(lax.axis_index("core") != giver)
    def _():
        out[...] = old[...].astype(BF)


def far_body(kind, rows_of, par, p1a, p1b, p2a, p2b, both, old, out):
    out[...] = old[...] + applied(par, rows_of(both), joined((p1a, p1b), (p2a, p2b), kind))


def image_end_body(par, old, given, unit, norm, whole, keep, send):
    dimg = par[0:1, 0:1] * (old[...] + given[...].astype(F32))
    value = unit[...]
    dproj = ((dimg - value * jnp.sum(value * dimg, -1, keepdims=True)) * norm[...]).astype(BF)
    whole[...] = dproj
    half = dproj.shape[1] // 2

    @pl.when(lax.axis_index("core") == 0)
    def _():
        keep[...] = dproj[:, :half]
        send[...] = dproj[:, half:]

    @pl.when(lax.axis_index("core") != 0)
    def _():
        keep[...] = dproj[:, half:]
        send[...] = dproj[:, :half]


def text_end_body(par, old, given, texts, out):
    dtxt = par[0:1, 0:1] * (old[...] + given[...].astype(F32))
    value, inverse = text_unit(texts[...])
    out[...] = (dtxt - value * jnp.sum(value * dtxt, -1, keepdims=True)) * inverse


TURNS = (0, 2, 1, 3)


def across_place():
    return lax.axis_index("x")


def along_place():
    return lax.axis_index("yh") * SIZES[4] + lax.axis_index("yl")


def place_of(first):
    return jnp.where(lax.axis_index("core") == first, across_place(), along_place())


def turned(place, pieces, outs):
    for turn, out in zip(TURNS, outs):
        out[...] = pieces[lax.rem(place + turn, 4)]


def head_own_body(keep, images, out):
    out[...] = mm(keep[...], images[...], (0, 0))


def head_body(base, other, images2, *rest):
    outs, pieces = rest[:4], rest[4]
    total = base[...] + mm(other[...], images2[...], (0, 0))
    rows, half = pieces.shape[1], total.shape[1] // 2

    @pl.when(lax.axis_index("core") == 0)
    def _():
        for k in range(4):
            pieces[k] = total[k * rows : (k + 1) * rows].astype(BF)

    @pl.when(lax.axis_index("core") != 0)
    def _():
        for k in range(4):
            up, left = 2 * (k // 2) * rows, (k % 2) * half
            first = total[up : up + rows, left : left + half]
            second = total[up + rows : up + 2 * rows, left : left + half]
            pieces[k] = jnp.concatenate([first, second], 1).astype(BF)

    turned(place_of(0), pieces, outs)


def quarter_body(a, b, c, d, *rest):
    outs, pieces = rest[:4], rest[4]
    total = a[...].astype(F32) + b[...].astype(F32) + c[...].astype(F32) + d[...].astype(F32)
    _, rows, half = pieces.shape

    def quadrant(down, right):
        return total[down * rows : (down + 1) * rows, right * half : (right + 1) * half].astype(BF)

    @pl.when(lax.axis_index("core") == 0)
    def _():
        for k in range(4):
            pieces[k] = quadrant(k // 2, k % 2)

    @pl.when(lax.axis_index("core") != 0)
    def _():
        for k in range(4):
            pieces[k] = quadrant(k % 2, k // 2)

    turned(place_of(1), pieces, outs)


def grad_image_body(dproj, head, out):
    out[...] = mm(dproj[...], head[...], (1, 1))


FOLD = 3


def folded(piece):
    rows = piece.shape[0] // FOLD
    return jnp.concatenate([piece[k * rows : (k + 1) * rows] for k in range(FOLD)], 1)


def unfolded(piece):
    width = piece.shape[1] // FOLD
    return jnp.concatenate([piece[:, k * width : (k + 1) * width] for k in range(FOLD)], 0)


def split_body(a, b, c, d, out):
    total = a[...].astype(F32) + b[...].astype(F32) + c[...].astype(F32) + d[...].astype(F32)
    own = out.shape[2] // FOLD
    for k in range(out.shape[0]):
        out[k] = folded(total[:, k * own : (k + 1) * own]).astype(BF)


def spread_body(parts, out):
    total = parts[0].astype(F32)
    for k in range(1, parts.shape[0]):
        total = total + parts[k].astype(F32)
    total = total.astype(BF)
    for k in range(out.shape[0]):
        out[k] = total


def join_body(factor, parts, out):
    yhs, xs, cores = SIZES[:3]
    order = [(yh * xs + x) * cores for x in range(xs) for yh in range(yhs)]
    order += [(yh * xs + x) * cores + 1 for yh in range(yhs) for x in range(xs)]
    out[...] = jnp.concatenate([unfolded(parts[k].astype(F32)) for k in order], 0).T * factor


def ring_pairs(turn, first):
    pairs = []
    for source in range(COUNT):
        yh, x, core, z, yl = np.unravel_index(source, SIZES)
        if core == first:
            x = (x + turn) % SIZES[1]
        else:
            y = (yh * SIZES[4] + yl + turn) % 4
            yh, yl = y // SIZES[4], y % SIZES[4]
        pairs.append((source, int(np.ravel_multi_index((yh, x, core, z, yl), SIZES))))
    return pairs


def on_device(images, texts, head, scale, bias):
    swap = core_pairs()
    count, width = images.shape
    half = width // 2
    big = (count, width)
    tie = lax.optimization_barrier

    part_of = ((count // 2, width), BF)
    par, p1a, p1b, p2a, p2b, both, unit_img, pnorm = call(
        start_body,
        [((2, 128), F32)] + [part_of] * 4 + [((3 * count, width), BF), (big, F32), ((count, 1), F32)],
        images, texts, head, scalars=(scale, bias), space=pltpu.HBM, limit=16,
        scratch=[
            pltpu.VMEM(big, BF), pltpu.VMEM(big, BF), pltpu.VMEM(head.shape, BF),
            pltpu.SemaphoreType.DMA((1 + len(CUTS),)),
        ],
    )
    ways = (mixed_pairs(0), mixed_pairs(1))
    near = [moved(p1a, ways[0]), moved(p2a, ways[1]), moved(p1b, ways[0]), moved(p2b, ways[1])]
    both_s = moved(both, swap)
    dimg, dtxt = call(home_body, [(big, F32)] * 2, par, both)
    near[0], dimg, dtxt = tie((near[0], dimg, dtxt))
    ordered, ordered2 = call(order_body, [(big, BF)] * 2, both, both_s)
    far = [moved(p, ways[k % 2]) for k, p in enumerate(near)]
    dimg, dtxt, dimg_s, dtxt_s = call(
        near_body, [(big, F32)] * 4, par, near[0], near[2], near[1], near[3], both, both_s, dimg, dtxt
    )
    far[0], far[1], dimg, dtxt, dimg_s, dtxt_s, ordered, ordered2 = tie(
        (far[0], far[1], dimg, dtxt, dimg_s, dtxt_s, ordered, ordered2)
    )
    (dimg_s,) = call(give_first_body, [(big, F32)], par, far[0], far[1], both_s, dimg_s)
    (dimg,) = call(far_half_body, [(big, F32)], par, far[0], far[1], both, dimg)
    far[2], far[3], dimg, dimg_s = tie((far[2], far[3], dimg, dimg_s))
    (give,) = call(give_last_body, [(big, BF)], par, far[2], far[3], both_s, dimg_s)
    given = moved(give, swap)
    (dimg,) = call(far_half_body, [(big, F32)], par, far[2], far[3], both, dimg)
    far = [far[0], far[2], far[1], far[3]]
    dproj, keep, send = call(
        image_end_body, [(big, BF), ((count, half), BF), ((count, half), BF)],
        par, dimg, given, unit_img, pnorm,
    )
    other = moved(send, swap)
    (base,) = call(head_own_body, [((half, width), F32)], keep, ordered)
    quarter = ((half // 4, width), BF)
    parts = call(
        head_body, [quarter] * 4, base, other, ordered2,
        scratch=[pltpu.VMEM((4, half // 4, width), BF)],
    )
    parts = list(parts)
    parts = parts[:1] + [moved(p, ring_pairs(t, 0)) for p, t in zip(parts[1:], TURNS[1:])]
    (grad_image,) = call(grad_image_body, [(big, F32)], dproj, head)
    (give,) = call(
        functools.partial(give_body, 0, 1, text_of), [(big, BF)], par, *far, both_s, dtxt_s
    )
    (dtxt,) = call(
        functools.partial(far_body, 1, text_of), [(big, F32)], par, *far, both, dtxt
    )
    given_txt = moved(give, swap)
    *parts, grad_image, given_txt, dtxt = tie((*parts, grad_image, given_txt, dtxt))
    small = ((half // 8, half), BF)
    parts = call(
        quarter_body, [small] * 4, *parts,
        scratch=[pltpu.VMEM((4, half // 8, half), BF)],
    )
    parts = list(parts)
    parts = parts[:1] + [moved(p, ring_pairs(t, 1)) for p, t in zip(parts[1:], TURNS[1:])]
    (grad_text,) = call(text_end_body, [(big, F32)], par, dtxt, given_txt, texts)
    *parts, grad_text = tie((*parts, grad_text))
    own = width // INNER
    (part,) = call(split_body, [((SIZES[3], half // 8 // FOLD, own * FOLD), BF)], *parts)
    part = lax.all_to_all(part, "z", 0, 0)
    (part,) = call(spread_body, [((BLKS, half // 8 // FOLD, own * FOLD), BF)], part)
    part = lax.all_to_all(part, ("yh", "x", "core"), 0, 0)
    factor = 1.0 / float(count * COUNT) ** 0.5
    (head_grad,) = call(functools.partial(join_body, factor), [((own, width), F32)], part)
    return (grad_image, grad_text, head_grad)


def solution(mesh):
    fine = Mesh(mesh.devices.reshape(SIZES), AXES)
    rows = P(AXES, None)
    return jax.shard_map(
        on_device,
        mesh=fine,
        in_specs=(rows, rows, P(), P(), P()),
        out_specs=(rows, rows, P(("z", "yl"), None)),
        check_vma=False,
    )
```

```python
import functools

import jax
import jax.numpy as jnp
import numpy as np
from jax import lax
from jax.experimental import pallas as pl
from jax.experimental.pallas import tpu as pltpu
from jax.sharding import Mesh, PartitionSpec as P

AXES = ("yh", "x", "core", "z", "yl")
SIZES = (2, 4, 2, 8, 2)
INNER = SIZES[3] * SIZES[4]
COUNT = 16 * INNER
CHIPS = SIZES[0] * SIZES[1]
BLKS = CHIPS * SIZES[2]
BF = jnp.bfloat16
F32 = jnp.float32


def chip_pairs(steps):
    shift = steps * SIZES[2] * INNER
    return [(source, (source + shift) % COUNT) for source in range(COUNT)]


def mixed_pairs(kind):
    ahead, back = chip_pairs(1), chip_pairs(-1)
    return [(ahead if (k // INNER) % 2 == kind else back)[k] for k in range(COUNT)]


def core_pairs(only=None):
    return [
        (source, source ^ INNER)
        for source in range(COUNT)
        if only is None or (source // INNER) % 2 == only
    ]


def moved(value, pairs):
    return lax.ppermute(value, AXES, pairs)


def mm(a, b, dims):
    return lax.dot_general(a, b, ((dims[:1], dims[1:]), ((), ())), preferred_element_type=F32)


def call(body, outs, *args, scalars=(), scratch=(), limit=8, space=pltpu.VMEM, small=0):
    in_specs = [pl.BlockSpec(memory_space=pltpu.SMEM)] * len(scalars)
    in_specs += [pl.BlockSpec(memory_space=space)] * len(args)
    shapes = [jax.ShapeDtypeStruct(shape, dtype) for shape, dtype in outs]
    if space is pltpu.HBM:
        args = [pltpu.with_memory_space_constraint(a, space) for a in args]
    return pl.pallas_call(
        body,
        out_shape=shapes,
        in_specs=in_specs,
        out_specs=[pl.BlockSpec(memory_space=pltpu.SMEM)] * small
        + [pl.BlockSpec(memory_space=pltpu.VMEM)] * (len(outs) - small),
        scratch_shapes=list(scratch),
        cost_estimate=pl.CostEstimate(
            flops=0,
            bytes_accessed=sum(int(np.prod(a.shape)) * a.dtype.itemsize for a in (*args, *shapes)),
            transcendentals=0,
        ),
        compiler_params=pltpu.CompilerParams(vmem_limit_bytes=limit * 2**20),
    )(*scalars, *args)


def sigmoid(x):
    return 1.0 / (1.0 + jnp.exp(-x))


def logits(par, rows, cols):
    return par[0:1, 0:1] * mm(rows, cols, (1, 1)) + par[1:2, 0:1]


def applied(par, rows, cols):
    logit = logits(par, rows, cols)
    return mm(sigmoid(logit).astype(BF), cols, (1, 0))


def text_unit(texts):
    tfloat = texts.astype(F32)
    tnorm = jnp.sqrt(jnp.sum(tfloat * tfloat, -1, keepdims=True) + 1e-06)
    inverse = 1.0 / tnorm
    return tfloat * inverse, inverse


CUTS = (0, 256, 512, 768, 1152)


def start_body(
    scale, bias, images, texts, head, par, own, rows, unit, norm, t_in, i_in, h_in, sems
):
    copies = [
        pltpu.make_async_copy(texts, t_in, sems.at[0]),
        pltpu.make_async_copy(images, i_in, sems.at[1]),
    ]
    for k in range(len(CUTS) - 1):
        part = pl.ds(CUTS[k], CUTS[k + 1] - CUTS[k])
        copies.append(pltpu.make_async_copy(head.at[part], h_in.at[part], sems.at[2 + k]))
    for copy in copies:
        copy.start()
    par[0:1] = jnp.full((1, par.shape[1]), scale[0], F32)
    par[1:2] = jnp.full((1, par.shape[1]), bias[0], F32)
    copies[0].wait()
    low_txt = text_unit(t_in[...])[0].astype(BF)
    copies[1].wait()
    proj = None
    for k in range(len(CUTS) - 1):
        copies[2 + k].wait()
        cut = slice(CUTS[k], CUTS[k + 1])
        term = jnp.dot(i_in[:, cut], h_in[cut, :], preferred_element_type=F32)
        proj = term if proj is None else proj + term
    inverse = 1.0 / jnp.sqrt(jnp.sum(proj * proj, -1, keepdims=True) + 1e-06)
    value = proj * inverse
    unit[...] = value
    norm[...] = inverse
    low = value.astype(BF)
    first = lax.axis_index("core") == 0
    own[...] = jnp.where(first, low_txt, low)
    rows[...] = jnp.where(first, low, low_txt)


def order_body(images, images_s, out, out_s):
    own = images.shape[1] // INNER
    for z in range(SIZES[3]):
        for yl in range(SIZES[4]):
            source, target = (z * SIZES[4] + yl) * own, (yl * SIZES[3] + z) * own
            out[:, target : target + own] = images[:, source : source + own]
            out_s[:, target : target + own] = images_s[:, source : source + own]


def home_body(par, own, rows, to_rows, to_own):
    logit = logits(par, rows[...], own[...])
    eye = lax.broadcasted_iota(jnp.int32, logit.shape, 0) == lax.broadcasted_iota(
        jnp.int32, logit.shape, 1
    )
    grad = jnp.where(eye, -sigmoid(-logit), sigmoid(logit)).astype(BF)
    to_rows[...] = mm(grad, own[...], (1, 0))
    to_own[...] = mm(grad, rows[...], (0, 0))


def near_body(par, block, own, rows, rows_s, to_rows, to_own, out_rows, out_own, out_s):
    out_rows[...] = to_rows[...] + applied(par, rows[...], block[...])
    out_own[...] = to_own[...] + applied(par, own[...], rows_s[...])
    out_s[...] = applied(par, rows_s[...], block[...])


def next_body(par, block, rows, rows_s, to_rows, to_s, out_rows, out_s):
    out_rows[...] = to_rows[...] + applied(par, rows[...], block[...])
    out_s[...] = to_s[...] + applied(par, rows_s[...], block[...])


def far_body(par, block, rows, old, out):
    out[...] = (old[...] + applied(par, rows[...], block[...])).astype(out.dtype)


def image_end_body(par, to_rows, to_own, given, unit, norm, whole, keep, send):
    whole_own = to_own[...] + given[...].astype(F32)
    first = lax.axis_index("core") == 0
    dimg = par[0:1, 0:1] * jnp.where(first, to_rows[...], whole_own)
    value = unit[...]
    dproj = ((dimg - value * jnp.sum(value * dimg, -1, keepdims=True)) * norm[...]).astype(BF)
    whole[...] = dproj
    half = dproj.shape[1] // 2

    @pl.when(lax.axis_index("core") == 0)
    def _():
        keep[...] = dproj[:, :half]
        send[...] = dproj[:, half:]

    @pl.when(lax.axis_index("core") != 0)
    def _():
        keep[...] = dproj[:, half:]
        send[...] = dproj[:, :half]


def text_end_body(par, to_rows, to_own, given, texts, out):
    whole_own = to_own[...] + given[...].astype(F32)
    first = lax.axis_index("core") == 0
    dtxt = par[0:1, 0:1] * jnp.where(first, whole_own, to_rows[...])
    value, inverse = text_unit(texts[...])
    out[...] = (dtxt - value * jnp.sum(value * dtxt, -1, keepdims=True)) * inverse


TURNS = ((0, 1, 2, 3), (0, 2, 1, 3))


def across_place():
    return lax.axis_index("x")


def along_place():
    return lax.axis_index("yh") * SIZES[4] + lax.axis_index("yl")


def place_of(first):
    return jnp.where(lax.axis_index("core") == first, across_place(), along_place())


def turned(stage, pieces, outs):
    place = place_of(stage)
    for turn, out in zip(TURNS[stage], outs):
        out[...] = pieces[lax.rem(place + turn, 4)]


def head_own_body(keep, images, out):
    out[...] = mm(keep[...], images[...], (0, 0))


def head_body(base, other, images2, *rest):
    outs, pieces = rest[:4], rest[4]
    total = base[...] + mm(other[...], images2[...], (0, 0))
    rows, half = pieces.shape[1], total.shape[1] // 2

    @pl.when(lax.axis_index("core") == 0)
    def _():
        for k in range(4):
            pieces[k] = total[k * rows : (k + 1) * rows].astype(BF)

    @pl.when(lax.axis_index("core") != 0)
    def _():
        for k in range(4):
            up, left = 2 * (k // 2) * rows, (k % 2) * half
            first = total[up : up + rows, left : left + half]
            second = total[up + rows : up + 2 * rows, left : left + half]
            pieces[k] = jnp.concatenate([first, second], 1).astype(BF)

    turned(0, pieces, outs)


def quarter_body(a, b, c, d, *rest):
    outs, pieces = rest[:4], rest[4]
    total = a[...].astype(F32) + b[...].astype(F32) + c[...].astype(F32) + d[...].astype(F32)
    _, rows, half = pieces.shape

    def quadrant(down, right):
        return total[down * rows : (down + 1) * rows, right * half : (right + 1) * half].astype(BF)

    @pl.when(lax.axis_index("core") == 0)
    def _():
        for k in range(4):
            pieces[k] = quadrant(k // 2, k % 2)

    @pl.when(lax.axis_index("core") != 0)
    def _():
        for k in range(4):
            pieces[k] = quadrant(k % 2, k // 2)

    turned(1, pieces, outs)


def grad_image_body(dproj, head, out):
    out[...] = mm(dproj[...], head[...], (1, 1))


FOLD = 3


def folded(piece):
    rows = piece.shape[0] // FOLD
    return jnp.concatenate([piece[k * rows : (k + 1) * rows] for k in range(FOLD)], 1)


def unfolded(piece):
    width = piece.shape[1] // FOLD
    return jnp.concatenate([piece[:, k * width : (k + 1) * width] for k in range(FOLD)], 0)


def split_body(a, b, c, d, out):
    total = a[...].astype(F32) + b[...].astype(F32) + c[...].astype(F32) + d[...].astype(F32)
    own = out.shape[2] // FOLD
    for k in range(out.shape[0]):
        out[k] = folded(total[:, k * own : (k + 1) * own]).astype(BF)


def spread_body(parts, out):
    total = parts[0].astype(F32)
    for k in range(1, parts.shape[0]):
        total = total + parts[k].astype(F32)
    total = total.astype(BF)
    for k in range(out.shape[0]):
        out[k] = total


def join_body(factor, parts, out):
    yhs, xs, cores = SIZES[:3]
    order = [(yh * xs + x) * cores for x in range(xs) for yh in range(yhs)]
    order += [(yh * xs + x) * cores + 1 for yh in range(yhs) for x in range(xs)]
    out[...] = jnp.concatenate([unfolded(parts[k].astype(F32)) for k in order], 0).T * factor


def ring_pairs(turn, first):
    pairs = []
    for source in range(COUNT):
        yh, x, core, z, yl = np.unravel_index(source, SIZES)
        if core == first:
            x = (x + turn) % SIZES[1]
        else:
            y = (yh * SIZES[4] + yl + turn) % 4
            yh, yl = y // SIZES[4], y % SIZES[4]
        pairs.append((source, int(np.ravel_multi_index((yh, x, core, z, yl), SIZES))))
    return pairs


def on_device(images, texts, head, scale, bias):
    swap = core_pairs()
    count, width = images.shape
    half = width // 2
    big = (count, width)
    tie = lax.optimization_barrier

    par, own, rows, unit_img, pnorm = call(
        start_body,
        [((2, 128), F32), (big, BF), (big, BF), (big, F32), ((count, 1), F32)],
        images, texts, head, scalars=(scale, bias), space=pltpu.HBM, limit=16,
        scratch=[
            pltpu.VMEM(big, BF), pltpu.VMEM(big, BF), pltpu.VMEM(head.shape, BF),
            pltpu.SemaphoreType.DMA((1 + len(CUTS),)),
        ],
    )
    way = mixed_pairs(0)
    near = moved(own, way)
    near_s = moved(moved(rows, swap), way)
    rows_s = moved(own, swap)
    images_s = moved(images, swap)
    to_rows, to_own = call(home_body, [(big, F32)] * 2, par, own, rows)
    near, to_rows, to_own = tie((near, to_rows, to_own))
    far = moved(near, way)
    to_rows, to_own, to_s = call(
        near_body, [(big, F32)] * 3, par, near, own, rows, rows_s, to_rows, to_own
    )
    near_s, to_rows, to_own, to_s = tie((near_s, to_rows, to_own, to_s))
    far_s = moved(near_s, way)
    to_rows, to_s = call(next_body, [(big, F32)] * 2, par, near_s, rows, rows_s, to_rows, to_s)
    ordered, ordered2 = call(order_body, [(big, BF)] * 2, images, images_s)
    far, to_rows, to_own, to_s, ordered, ordered2 = tie(
        (far, to_rows, to_own, to_s, ordered, ordered2)
    )
    (to_rows,) = call(far_body, [(big, F32)], par, far, rows, to_rows)
    far_s, to_rows = tie((far_s, to_rows))
    (give,) = call(far_body, [(big, BF)], par, far_s, rows_s, to_s)
    given = moved(give, swap)
    (to_rows,) = call(far_body, [(big, F32)], par, far_s, rows, to_rows)
    dproj, keep, send = call(
        image_end_body, [(big, BF), ((count, half), BF), ((count, half), BF)],
        par, to_rows, to_own, given, unit_img, pnorm,
    )
    other = moved(send, swap)
    (base,) = call(head_own_body, [((half, width), F32)], keep, ordered)
    quarter = ((half // 4, width), BF)
    parts = call(
        head_body, [quarter] * 4, base, other, ordered2,
        scratch=[pltpu.VMEM((4, half // 4, width), BF)],
    )
    parts = list(parts)
    parts = parts[:1] + [moved(p, ring_pairs(t, 0)) for p, t in zip(parts[1:], TURNS[0][1:])]
    (grad_image,) = call(grad_image_body, [(big, F32)], dproj, head)
    (grad_text,) = call(text_end_body, [(big, F32)], par, to_rows, to_own, given, texts)
    *parts, grad_image, grad_text = tie((*parts, grad_image, grad_text))
    small = ((half // 8, half), BF)
    parts = call(
        quarter_body, [small] * 4, *parts,
        scratch=[pltpu.VMEM((4, half // 8, half), BF)],
    )
    parts = list(parts)
    parts = parts[:1] + [moved(p, ring_pairs(t, 1)) for p, t in zip(parts[1:], TURNS[1][1:])]
    own = width // INNER
    (part,) = call(split_body, [((SIZES[3], half // 8 // FOLD, own * FOLD), BF)], *parts)
    part = lax.all_to_all(part, "z", 0, 0)
    (part,) = call(spread_body, [((BLKS, half // 8 // FOLD, own * FOLD), BF)], part)
    part = lax.all_to_all(part, ("yh", "x", "core"), 0, 0)
    factor = 1.0 / float(count * COUNT) ** 0.5
    (head_grad,) = call(functools.partial(join_body, factor), [((own, width), F32)], part)
    return (grad_image, grad_text, head_grad)


def solution(mesh):
    fine = Mesh(mesh.devices.reshape(SIZES), AXES)
    rows = P(AXES, None)
    return jax.shard_map(
        on_device,
        mesh=fine,
        in_specs=(rows, rows, P(), P(), P()),
        out_specs=(rows, rows, P(("z", "yl"), None)),
        check_vma=False,
    )
```

```python
import functools

import jax
import jax.numpy as jnp
import numpy as np
from jax import lax
from jax.experimental import pallas as pl
from jax.experimental.pallas import tpu as pltpu
from jax.sharding import Mesh, PartitionSpec as P

AXES = ("yh", "x", "core", "z", "yl")
SIZES = (2, 4, 2, 8, 2)
INNER = SIZES[3] * SIZES[4]
COUNT = 16 * INNER
CHIPS = SIZES[0] * SIZES[1]
BLKS = CHIPS * SIZES[2]
BF = jnp.bfloat16
F32 = jnp.float32


def chip_pairs(steps):
    shift = steps * SIZES[2] * INNER
    return [(source, (source + shift) % COUNT) for source in range(COUNT)]


def mixed_pairs(kind):
    ahead, back = chip_pairs(1), chip_pairs(-1)
    return [(ahead if (k // INNER) % 2 == kind else back)[k] for k in range(COUNT)]


def core_pairs(only=None):
    return [
        (source, source ^ INNER)
        for source in range(COUNT)
        if only is None or (source // INNER) % 2 == only
    ]


def moved(value, pairs):
    return lax.ppermute(value, AXES, pairs)


def mm(a, b, dims):
    return lax.dot_general(a, b, ((dims[:1], dims[1:]), ((), ())), preferred_element_type=F32)


def call(body, outs, *args, scalars=(), scratch=(), limit=8, space=pltpu.VMEM, small=0):
    in_specs = [pl.BlockSpec(memory_space=pltpu.SMEM)] * len(scalars)
    in_specs += [pl.BlockSpec(memory_space=space)] * len(args)
    shapes = [jax.ShapeDtypeStruct(shape, dtype) for shape, dtype in outs]
    if space is pltpu.HBM:
        args = [pltpu.with_memory_space_constraint(a, space) for a in args]
    return pl.pallas_call(
        body,
        out_shape=shapes,
        in_specs=in_specs,
        out_specs=[pl.BlockSpec(memory_space=pltpu.SMEM)] * small
        + [pl.BlockSpec(memory_space=pltpu.VMEM)] * (len(outs) - small),
        scratch_shapes=list(scratch),
        cost_estimate=pl.CostEstimate(
            flops=0,
            bytes_accessed=sum(int(np.prod(a.shape)) * a.dtype.itemsize for a in (*args, *shapes)),
            transcendentals=0,
        ),
        compiler_params=pltpu.CompilerParams(vmem_limit_bytes=limit * 2**20),
    )(*scalars, *args)


def sigmoid(x):
    return 1.0 / (1.0 + jnp.exp(-x))


def logits(par, rows, cols):
    return par[0:1, 0:1] * mm(rows, cols, (1, 1)) + par[1:2, 0:1]


def applied(par, rows, cols):
    logit = logits(par, rows, cols)
    return mm(sigmoid(logit).astype(BF), cols, (1, 0))


def text_unit(texts):
    tfloat = texts.astype(F32)
    tnorm = jnp.sqrt(jnp.sum(tfloat * tfloat, -1, keepdims=True) + 1e-06)
    inverse = 1.0 / tnorm
    return tfloat * inverse, inverse


def halved(value, first, second):
    rows = value.shape[0] // 2
    first[...] = value[:rows]
    second[...] = value[rows:]


CUTS = (0, 256, 512, 768, 1152)


def start_body(
    scale, bias, images, texts, head, par,
    p1a, p1b, p2a, p2b, both, unit, norm, t_in, i_in, h_in, sems,
):
    copies = [
        pltpu.make_async_copy(texts, t_in, sems.at[0]),
        pltpu.make_async_copy(images, i_in, sems.at[1]),
    ]
    for k in range(len(CUTS) - 1):
        rows = pl.ds(CUTS[k], CUTS[k + 1] - CUTS[k])
        copies.append(pltpu.make_async_copy(head.at[rows], h_in.at[rows], sems.at[2 + k]))
    for copy in copies:
        copy.start()
    par[0:1] = jnp.full((1, par.shape[1]), scale[0], F32)
    par[1:2] = jnp.full((1, par.shape[1]), bias[0], F32)
    copies[0].wait()
    count = t_in.shape[0]
    low = text_unit(t_in[...])[0].astype(BF)
    both[:count] = low
    low_txt = low
    copies[1].wait()
    both[2 * count :] = i_in[...]
    proj = None
    for k in range(len(CUTS) - 1):
        copies[2 + k].wait()
        cut = slice(CUTS[k], CUTS[k + 1])
        term = jnp.dot(i_in[:, cut], h_in[cut, :], preferred_element_type=F32)
        proj = term if proj is None else proj + term
    inverse = 1.0 / jnp.sqrt(jnp.sum(proj * proj, -1, keepdims=True) + 1e-06)
    value = proj * inverse
    unit[...] = value
    norm[...] = inverse
    low = value.astype(BF)
    both[count : 2 * count] = low

    @pl.when(lax.axis_index("core") == 0)
    def _():
        halved(low_txt, p1a, p1b)
        halved(low, p2a, p2b)

    @pl.when(lax.axis_index("core") != 0)
    def _():
        halved(low, p1a, p1b)
        halved(low_txt, p2a, p2b)


def text_of(both):
    return both[: both.shape[0] // 3]


def image_of(both):
    count = both.shape[0] // 3
    return both[count : 2 * count]


def order_body(both, both_s, out, out2):
    own = both.shape[1] // INNER
    count = both.shape[0] // 3
    for z in range(SIZES[3]):
        for yl in range(SIZES[4]):
            source, target = (z * SIZES[4] + yl) * own, (yl * SIZES[3] + z) * own
            out[:, target : target + own] = both[2 * count :, source : source + own]
            out2[:, target : target + own] = both_s[2 * count :, source : source + own]


def home_body(par, both, dimg, dtxt):
    img_b, txt_b = image_of(both), text_of(both)
    logit = logits(par, img_b, txt_b)
    eye = lax.broadcasted_iota(jnp.int32, logit.shape, 0) == lax.broadcasted_iota(
        jnp.int32, logit.shape, 1
    )
    grad = jnp.where(eye, -sigmoid(-logit), sigmoid(logit)).astype(BF)
    dimg[...] = mm(grad, txt_b, (1, 0))
    dtxt[...] = mm(grad, img_b, (0, 0))


def joined(one, two, kind):
    here = lax.axis_index("core") == kind
    return jnp.concatenate([jnp.where(here, a[...], b[...]) for a, b in zip(one, two)], 0)


def near_body(par, p1a, p1b, p2a, p2b, both, both_s, dimg, dtxt, dimg_o, dtxt_o, dimg_s, dtxt_s):
    t1, i1 = (joined((p1a, p1b), (p2a, p2b), kind) for kind in range(2))
    dimg_o[...] = dimg[...] + applied(par, image_of(both), t1)
    dtxt_o[...] = dtxt[...] + applied(par, text_of(both), i1)
    dimg_s[...] = applied(par, image_of(both_s), t1)
    dtxt_s[...] = applied(par, text_of(both_s), i1)

    @pl.when(lax.axis_index("core") == 0)
    def _():
        dtxt_o[...] += applied(par, text_of(both), image_of(both_s))

    @pl.when(lax.axis_index("core") != 0)
    def _():
        dimg_o[...] += applied(par, image_of(both), text_of(both_s))


def give_body(giver, kind, rows_of, par, p1a, p1b, p2a, p2b, both_s, old, out):
    @pl.when(lax.axis_index("core") == giver)
    def _():
        out[...] = (old[...] + applied(par, rows_of(both_s), joined((p1a, p1b), (p2a, p2b), kind))).astype(BF)

    @pl.when(lax.axis_index("core") != giver)
    def _():
        out[...] = old[...].astype(BF)


def far_body(kind, rows_of, par, p1a, p1b, p2a, p2b, both, old, out):
    out[...] = old[...] + applied(par, rows_of(both), joined((p1a, p1b), (p2a, p2b), kind))


def image_end_body(par, old, given, unit, norm, whole, keep, send):
    dimg = par[0:1, 0:1] * (old[...] + given[...].astype(F32))
    value = unit[...]
    dproj = ((dimg - value * jnp.sum(value * dimg, -1, keepdims=True)) * norm[...]).astype(BF)
    whole[...] = dproj
    half = dproj.shape[1] // 2

    @pl.when(lax.axis_index("core") == 0)
    def _():
        keep[...] = dproj[:, :half]
        send[...] = dproj[:, half:]

    @pl.when(lax.axis_index("core") != 0)
    def _():
        keep[...] = dproj[:, half:]
        send[...] = dproj[:, :half]


def text_end_body(par, old, given, texts, out):
    dtxt = par[0:1, 0:1] * (old[...] + given[...].astype(F32))
    value, inverse = text_unit(texts[...])
    out[...] = (dtxt - value * jnp.sum(value * dtxt, -1, keepdims=True)) * inverse


TURNS = (0, 2, 1, 3)


def across_place():
    return lax.axis_index("x")


def along_place():
    return lax.axis_index("yh") * SIZES[4] + lax.axis_index("yl")


def place_of(first):
    return jnp.where(lax.axis_index("core") == first, across_place(), along_place())


def turned(place, pieces, outs):
    for turn, out in zip(TURNS, outs):
        out[...] = pieces[lax.rem(place + turn, 4)]


def head_own_body(keep, images, out):
    out[...] = mm(keep[...], images[...], (0, 0))


def head_body(base, other, images2, *rest):
    outs, pieces = rest[:4], rest[4]
    total = base[...] + mm(other[...], images2[...], (0, 0))
    rows, half = pieces.shape[1], total.shape[1] // 2

    @pl.when(lax.axis_index("core") == 0)
    def _():
        for k in range(4):
            pieces[k] = total[k * rows : (k + 1) * rows].astype(BF)

    @pl.when(lax.axis_index("core") != 0)
    def _():
        for k in range(4):
            up, left = 2 * (k // 2) * rows, (k % 2) * half
            first = total[up : up + rows, left : left + half]
            second = total[up + rows : up + 2 * rows, left : left + half]
            pieces[k] = jnp.concatenate([first, second], 1).astype(BF)

    turned(place_of(0), pieces, outs)


def quarter_body(a, b, c, d, *rest):
    outs, pieces = rest[:4], rest[4]
    total = a[...].astype(F32) + b[...].astype(F32) + c[...].astype(F32) + d[...].astype(F32)
    _, rows, half = pieces.shape

    def quadrant(down, right):
        return total[down * rows : (down + 1) * rows, right * half : (right + 1) * half].astype(BF)

    @pl.when(lax.axis_index("core") == 0)
    def _():
        for k in range(4):
            pieces[k] = quadrant(k // 2, k % 2)

    @pl.when(lax.axis_index("core") != 0)
    def _():
        for k in range(4):
            pieces[k] = quadrant(k % 2, k // 2)

    turned(place_of(1), pieces, outs)


def grad_image_body(dproj, head, out):
    out[...] = mm(dproj[...], head[...], (1, 1))


FOLD = 3


def folded(piece):
    rows = piece.shape[0] // FOLD
    return jnp.concatenate([piece[k * rows : (k + 1) * rows] for k in range(FOLD)], 1)


def unfolded(piece):
    width = piece.shape[1] // FOLD
    return jnp.concatenate([piece[:, k * width : (k + 1) * width] for k in range(FOLD)], 0)


def split_body(a, b, c, d, out):
    total = a[...].astype(F32) + b[...].astype(F32) + c[...].astype(F32) + d[...].astype(F32)
    own = out.shape[2] // FOLD
    for k in range(out.shape[0]):
        out[k] = folded(total[:, k * own : (k + 1) * own]).astype(BF)


def spread_body(parts, out):
    total = parts[0].astype(F32)
    for k in range(1, parts.shape[0]):
        total = total + parts[k].astype(F32)
    total = total.astype(BF)
    for k in range(out.shape[0]):
        out[k] = total


def join_body(factor, parts, out):
    yhs, xs, cores = SIZES[:3]
    order = [(yh * xs + x) * cores for x in range(xs) for yh in range(yhs)]
    order += [(yh * xs + x) * cores + 1 for yh in range(yhs) for x in range(xs)]
    out[...] = jnp.concatenate([unfolded(parts[k].astype(F32)) for k in order], 0).T * factor


def ring_pairs(turn, first):
    pairs = []
    for source in range(COUNT):
        yh, x, core, z, yl = np.unravel_index(source, SIZES)
        if core == first:
            x = (x + turn) % SIZES[1]
        else:
            y = (yh * SIZES[4] + yl + turn) % 4
            yh, yl = y // SIZES[4], y % SIZES[4]
        pairs.append((source, int(np.ravel_multi_index((yh, x, core, z, yl), SIZES))))
    return pairs


def on_device(images, texts, head, scale, bias):
    swap = core_pairs()
    count, width = images.shape
    half = width // 2
    big = (count, width)
    tie = lax.optimization_barrier

    part_of = ((count // 2, width), BF)
    par, p1a, p1b, p2a, p2b, both, unit_img, pnorm = call(
        start_body,
        [((2, 128), F32)] + [part_of] * 4 + [((3 * count, width), BF), (big, F32), ((count, 1), F32)],
        images, texts, head, scalars=(scale, bias), space=pltpu.HBM, limit=16,
        scratch=[
            pltpu.VMEM(big, BF), pltpu.VMEM(big, BF), pltpu.VMEM(head.shape, BF),
            pltpu.SemaphoreType.DMA((1 + len(CUTS),)),
        ],
    )
    ways = (mixed_pairs(0), mixed_pairs(1))
    near = [moved(p1a, ways[0]), moved(p2a, ways[1]), moved(p1b, ways[0]), moved(p2b, ways[1])]
    both_s = moved(both, swap)
    dimg, dtxt = call(home_body, [(big, F32)] * 2, par, both)
    near[0], dimg, dtxt = tie((near[0], dimg, dtxt))
    ordered, ordered2 = call(order_body, [(big, BF)] * 2, both, both_s)
    far = [moved(p, ways[k % 2]) for k, p in enumerate(near)]
    dimg, dtxt, dimg_s, dtxt_s = call(
        near_body, [(big, F32)] * 4, par, near[0], near[2], near[1], near[3], both, both_s, dimg, dtxt
    )
    *far, dimg, dtxt, dimg_s, dtxt_s, ordered, ordered2 = tie(
        (*far, dimg, dtxt, dimg_s, dtxt_s, ordered, ordered2)
    )
    far = [far[0], far[2], far[1], far[3]]

    (give,) = call(
        functools.partial(give_body, 1, 0, image_of), [(big, BF)], par, *far, both_s, dimg_s
    )
    given = moved(give, swap)
    (dimg,) = call(
        functools.partial(far_body, 0, image_of), [(big, F32)], par, *far, both, dimg
    )
    dproj, keep, send = call(
        image_end_body, [(big, BF), ((count, half), BF), ((count, half), BF)],
        par, dimg, given, unit_img, pnorm,
    )
    other = moved(send, swap)
    (base,) = call(head_own_body, [((half, width), F32)], keep, ordered)
    quarter = ((half // 4, width), BF)
    parts = call(
        head_body, [quarter] * 4, base, other, ordered2,
        scratch=[pltpu.VMEM((4, half // 4, width), BF)],
    )
    parts = list(parts)
    parts = parts[:1] + [moved(p, ring_pairs(t, 0)) for p, t in zip(parts[1:], TURNS[1:])]
    (grad_image,) = call(grad_image_body, [(big, F32)], dproj, head)
    (give,) = call(
        functools.partial(give_body, 0, 1, text_of), [(big, BF)], par, *far, both_s, dtxt_s
    )
    (dtxt,) = call(
        functools.partial(far_body, 1, text_of), [(big, F32)], par, *far, both, dtxt
    )
    given_txt = moved(give, swap)
    *parts, grad_image, given_txt, dtxt = tie((*parts, grad_image, given_txt, dtxt))
    small = ((half // 8, half), BF)
    parts = call(
        quarter_body, [small] * 4, *parts,
        scratch=[pltpu.VMEM((4, half // 8, half), BF)],
    )
    parts = list(parts)
    parts = parts[:1] + [moved(p, ring_pairs(t, 1)) for p, t in zip(parts[1:], TURNS[1:])]
    (grad_text,) = call(text_end_body, [(big, F32)], par, dtxt, given_txt, texts)
    *parts, grad_text = tie((*parts, grad_text))
    own = width // INNER
    (part,) = call(split_body, [((SIZES[3], half // 8 // FOLD, own * FOLD), BF)], *parts)
    part = lax.all_to_all(part, "z", 0, 0)
    (part,) = call(spread_body, [((BLKS, half // 8 // FOLD, own * FOLD), BF)], part)
    part = lax.all_to_all(part, ("yh", "x", "core"), 0, 0)
    factor = 1.0 / float(count * COUNT) ** 0.5
    (head_grad,) = call(functools.partial(join_body, factor), [((own, width), F32)], part)
    return (grad_image, grad_text, head_grad)


def solution(mesh):
    fine = Mesh(mesh.devices.reshape(SIZES), AXES)
    rows = P(AXES, None)
    return jax.shard_map(
        on_device,
        mesh=fine,
        in_specs=(rows, rows, P(), P(), P()),
        out_specs=(rows, rows, P(("z", "yl"), None)),
        check_vma=False,
    )
```
